256 devices in a mesh: pipe: 8 (over x_hi, y), expert: 32 (over x_lo, z, core).
Axes of the slice: x: 4 (x_hi: 2, x_lo: 2; x = x_hi * 2 + x_lo), y: 4, z: 8, core: 2. Of those that a mesh axis runs over, the one named last changes fastest.
Arguments:
- hidden_a: bfloat16 [8, 4096, 2048], P('pipe', 'expert'), may hold values from -4.5 to 4.5
- expert_ids_a: int32 [8, 4096, 8], P('pipe', 'expert'), may hold values from 0 to 127, as said below
- router_probs_a: float32 [8, 4096, 8], P('pipe', 'expert'), may hold values from 0.02 to 1
- hidden_b: bfloat16 [8, 4096, 2048], P('pipe', 'expert'), may hold values from -4.5 to 4.5
- expert_ids_b: int32 [8, 4096, 8], P('pipe', 'expert'), may hold values from 0 to 127, as said below
- router_probs_b: float32 [8, 4096, 8], P('pipe', 'expert'), may hold values from 0.02 to 1
- grad_out_b: bfloat16 [8, 4096, 2048], P('pipe', 'expert'), may hold values from -6 to 6
- norm_gain: float32 [8, 2048], P('pipe'), may hold values from 0.5 to 2
- w_gate: bfloat16 [8, 32, 2048, 768], P('pipe', 'expert'), may hold values from -0.125 to 0.125
- w_up: bfloat16 [8, 32, 2048, 768], P('pipe', 'expert'), may hold values from -0.125 to 0.125
- w_down: bfloat16 [8, 32, 768, 2048], P('pipe', 'expert'), may hold values from -0.21875 to 0.21875
Outputs:
- next_hidden_a: bfloat16 [8, 4096, 2048], P('pipe', 'expert')
- grad_in_b: bfloat16 [8, 4096, 2048], P('pipe', 'expert')
The draws below stay inside these ranges and needn't reach their ends.
Inputs may be any that keep to these rules, and one draw needn't show every extreme that they name: `expert_ids_a`: position k of every token names an expert of k * 16 to (k + 1) * 16 - 1. In each aligned block of 128 tokens (the tokens of one device), for each position one expert (the hot one) is named by exactly 16 tokens; it is the same in all blocks and sections and in both micro-batches, and for position 0 it lies below min(16, 32). Every other expert is named by at most 8 tokens of a block, and in every block and position one of them by exactly 8. `expert_ids_b`: position k of every token names an expert of k * 16 to (k + 1) * 16 - 1. In each aligned block of 128 tokens (the tokens of one device), for each position one expert (the hot one) is named by exactly 16 tokens; it is the same in all blocks and sections and in both micro-batches, and for position 0 it lies below min(16, 32). Every other expert is named by at most 8 tokens of a block, and in every block and position one of them by exactly 8.
All inputs are finite; a program needn't handle non-finite values.
Results may differ from the reference program's by a relative error of at most 0.0066.
Values may be sent and summed in bfloat16 or wider, within the bound.
A program may use at most 128 MiB of HBM per device.

```python
import math
import jax
import jax.numpy as jnp
from jax import lax

D = 2048
FF = 768
TOP = 8
TOK_DEV = 128
SECTIONS = 8
EXP_GROUP = 16
WIN_EXP = 32
CAP = 16
TOKENS = 4096
N_EXPERT = 32


def scaled_field(key_scale, base_draw):
    key_rows, key_cols = jax.random.split(key_scale, 2)
    row_scale = jnp.exp(jax.random.uniform(key_rows, (SECTIONS, TOKENS, 1), jnp.float32, math.log(0.05), math.log(0.5)))
    col_scale = jnp.exp(jax.random.uniform(key_cols, (SECTIONS, 1, D), jnp.float32, math.log(0.3), math.log(3.0)))
    return (base_draw * row_scale * col_scale).astype(jnp.bfloat16)


def draw_hidden_a(key, part):
    key = jax.random.fold_in(key, 11)
    key_base, key_scale = jax.random.split(key)
    base_draw = jax.random.truncated_normal(key_base, -3.0, 3.0, (SECTIONS, TOKENS, D), jnp.float32)
    return scaled_field(key_scale, base_draw)


def draw_hidden_b(key, part):
    key = jax.random.fold_in(key, 12)
    key_base, key_scale = jax.random.split(key)
    base_draw = jax.random.truncated_normal(key_base, -3.0, 3.0, (SECTIONS, TOKENS, D), jnp.float32)
    return scaled_field(key_scale, base_draw)


def shared_hot(key):
    key_first, key_hot = jax.random.split(key)
    first_hot = jax.random.randint(key_first, (1,), 0, min(EXP_GROUP, WIN_EXP))
    other_hot = jax.random.randint(key_hot, (TOP - 1,), 0, EXP_GROUP)
    return jnp.concatenate([first_hot, other_hot]).astype(jnp.int32)


def group_routes(key_routes, hot_ids):
    block_count = SECTIONS * TOKENS // TOK_DEV
    half_cap = CAP // 2
    pool_size = (EXP_GROUP - 2) * half_cap
    rest = TOK_DEV - CAP - half_cap
    key_second, key_pool, key_place = jax.random.split(key_routes, 3)
    second_offset = jax.random.randint(key_second, (block_count, TOP), 0, EXP_GROUP - 1).astype(jnp.int32)
    pool_keys = jax.random.split(key_pool, block_count * TOP)
    pool_draws = jax.vmap(lambda one_key: jax.random.permutation(one_key, pool_size))(pool_keys)
    pool_draws = pool_draws.reshape(block_count, TOP, pool_size)[:, :, :rest]
    index_other = (pool_draws // half_cap).astype(jnp.int32)
    offset_other = index_other + (index_other >= second_offset[:, :, None]).astype(jnp.int32)
    others = (hot_ids[None, :, None] + 1 + offset_other) % EXP_GROUP
    second_ids = (hot_ids[None, :] + 1 + second_offset) % EXP_GROUP
    second_slots = jnp.broadcast_to(second_ids[:, :, None], (block_count, TOP, half_cap))
    hot_slots = jnp.broadcast_to(hot_ids[None, :, None], (block_count, TOP, CAP))
    ordered = jnp.concatenate([hot_slots, second_slots, others], axis=2)
    place_keys = jax.random.split(key_place, block_count * TOP)
    places = jax.vmap(lambda one_key: jax.random.permutation(one_key, TOK_DEV))(place_keys)
    places = places.reshape(block_count, TOP, TOK_DEV)
    within = jnp.take_along_axis(ordered, places, axis=2)
    offsets = (jnp.arange(TOP, dtype=jnp.int32) * EXP_GROUP)[None, :, None]
    chosen = jnp.transpose(within + offsets, (0, 2, 1))
    return chosen.reshape(SECTIONS, TOKENS, TOP).astype(jnp.int32)


def draw_expert_ids_a(key, part):
    hot_ids = shared_hot(key)
    key = jax.random.fold_in(key, 21)
    return group_routes(key, hot_ids)


def draw_expert_ids_b(key, part):
    hot_ids = shared_hot(key)
    key = jax.random.fold_in(key, 22)
    return group_routes(key, hot_ids)


def steps_of(rng, shape, shards, smallest, high):
    def one(dim, blocks):
        draws = jax.random.uniform(jax.random.fold_in(jax.random.fold_in(rng, 6), dim), (blocks,), jnp.float32, smallest / len(shards), high / len(shards))
        return jnp.repeat(jnp.exp(draws), shape[dim] // blocks).reshape((-1,) + (1,) * (len(shape) - dim - 1))

    loudness = one(*shards[0])
    for cut in shards[1:]:
        loudness = loudness * one(*cut)
    return loudness


def centred(rng, shape, spread, limit, shards=(), kind=jnp.bfloat16):
    result = spread * jax.random.normal(rng, shape, jnp.float32)
    if shards:
        result = result * steps_of(rng, shape, shards, -0.22, 0.18)
    return jnp.clip(result, -limit, limit).astype(kind)


def setup_inputs(seed: int = 0) -> dict:
    splits = jax.random.split(jax.random.key(seed), 12)
    hidden_a = draw_hidden_a(jax.random.fold_in(splits[11], 71), 0)
    expert_ids_a = draw_expert_ids_a(jax.random.fold_in(splits[11], 71), 0)
    router_probs_a = jnp.clip(jnp.exp(math.log(1.0) - 3.912023 * jax.random.uniform(splits[2], (SECTIONS, TOKENS, TOP), jnp.float32) ** steps_of(splits[2], (SECTIONS, TOKENS, TOP), ((0, 8), (1, 32)), -0.2, 0.2)), 0.02, 1.0)
    hidden_b = draw_hidden_b(jax.random.fold_in(splits[11], 71), 0)
    expert_ids_b = draw_expert_ids_b(jax.random.fold_in(splits[11], 71), 0)
    router_probs_b = jnp.clip(jnp.exp(math.log(1.0) - 3.912023 * jax.random.uniform(splits[5], (SECTIONS, TOKENS, TOP), jnp.float32) ** steps_of(splits[5], (SECTIONS, TOKENS, TOP), ((0, 8), (1, 32)), -0.2, 0.2)), 0.02, 1.0)
    grad_out_b = centred(splits[6], (SECTIONS, TOKENS, D), 1.0, 6.0, ((0, 8), (1, 32)))
    norm_gain = jnp.clip(jnp.exp(math.log(2.0) - 1.3862944 * jax.random.uniform(splits[7], (SECTIONS, D), jnp.float32) ** steps_of(splits[7], (SECTIONS, D), ((0, 8),), -0.2, 0.2)), 0.5, 2.0)
    w_gate = centred(splits[8], (SECTIONS, WIN_EXP, D, FF), D ** -0.5, 0.125, ((0, 8), (1, 32)))
    w_up = centred(splits[9], (SECTIONS, WIN_EXP, D, FF), D ** -0.5, 0.125, ((0, 8), (1, 32)))
    w_down = centred(splits[10], (SECTIONS, WIN_EXP, FF, D), FF ** -0.5, 0.21875, ((0, 8), (1, 32)))
    return {"hidden_a": hidden_a, "expert_ids_a": expert_ids_a, "router_probs_a": router_probs_a, "hidden_b": hidden_b, "expert_ids_b": expert_ids_b, "router_probs_b": router_probs_b, "grad_out_b": grad_out_b, "norm_gain": norm_gain, "w_gate": w_gate, "w_up": w_up, "w_down": w_down}


NORM_EPS = 1e-06

def normed_rows(values, gain_row):
    as_float = values.astype(jnp.float32)
    inverse = lax.rsqrt(lax.optimization_barrier(jnp.mean(as_float * as_float, axis=-1, keepdims=True)) + NORM_EPS)
    return as_float * inverse * gain_row

def route_table(expert_ids, experts_here, capacity):
    inside = expert_ids < experts_here
    matches = (expert_ids[:, :, None] == jnp.arange(experts_here, dtype=jnp.int32)[None, None, :]).astype(jnp.int32)
    per_token = lax.optimization_barrier(jnp.sum(matches, axis=1))
    earlier = jnp.cumsum(per_token, axis=0) - per_token
    slot_index = lax.optimization_barrier(jnp.sum(matches * earlier[:, None, :], axis=2))
    target = jnp.where(inside, expert_ids * capacity + slot_index, experts_here * capacity).astype(jnp.int32)
    return (inside, target)

def slot_sources(target, experts_here, capacity):
    token_count, top_count = target.shape
    pair_index = jnp.arange(token_count * top_count, dtype=jnp.int32)
    slot_table = jnp.full((experts_here * capacity + 1,), token_count * top_count, jnp.int32)
    slot_table = slot_table.at[target.reshape(-1)].set(pair_index)
    return slot_table[:experts_here * capacity]

def pad_zero_row(values):
    return jnp.concatenate([values, jnp.zeros((1, values.shape[1]), values.dtype)], axis=0)

def dispatch_rows(normed, sources, top_count, experts_here):
    tokens_of = (sources // top_count).astype(jnp.int32)
    return pad_zero_row(normed)[tokens_of].reshape(experts_here, -1, normed.shape[1])

def scaled_rows(gradients, weight, sources, experts_here):
    top_count = weight.shape[1]
    flat_weight = jnp.concatenate([weight.reshape(-1), jnp.zeros((1,), weight.dtype)])
    tokens_of = (sources // top_count).astype(jnp.int32)
    picked = flat_weight[sources][:, None] * pad_zero_row(gradients)[tokens_of].astype(jnp.float32)
    return picked.astype(jnp.bfloat16).reshape(experts_here, -1, gradients.shape[1])

def contract_last(left, right):
    return lax.dot_general(left, right, (((1,), (1,)), ((), ())), preferred_element_type=jnp.float32)

def expert_forward(rows_in, gate_matrix, up_matrix, down_matrix):
    gate_pre = jnp.dot(rows_in, gate_matrix, preferred_element_type=jnp.float32)
    up_pre = jnp.dot(rows_in, up_matrix, preferred_element_type=jnp.float32)
    hidden_units = (gate_pre * jax.nn.sigmoid(gate_pre) * up_pre).astype(jnp.bfloat16)
    return jnp.dot(hidden_units, down_matrix, preferred_element_type=jnp.float32).astype(jnp.bfloat16)

def expert_backward(rows_in, upstream, gate_matrix, up_matrix, down_matrix):
    gate_pre = jnp.dot(rows_in, gate_matrix, preferred_element_type=jnp.float32)
    up_pre = jnp.dot(rows_in, up_matrix, preferred_element_type=jnp.float32)
    sigmoid_gate = jax.nn.sigmoid(gate_pre)
    d_hidden = contract_last(upstream, down_matrix)
    d_gate = (d_hidden * up_pre * sigmoid_gate * (1.0 + gate_pre * (1.0 - sigmoid_gate))).astype(jnp.bfloat16)
    d_up = (d_hidden * gate_pre * sigmoid_gate).astype(jnp.bfloat16)
    summed = contract_last(d_gate, gate_matrix) + contract_last(d_up, up_matrix)
    return summed.astype(jnp.bfloat16)

def combine_rows(start_rows, weight, inside, target, returned):
    padded = pad_zero_row(returned.reshape(-1, returned.shape[-1]))
    kept_weight = jnp.where(inside, weight, jnp.zeros_like(weight))
    running = start_rows
    for position in range(target.shape[1]):
        running = running + kept_weight[:, position:position + 1] * padded[target[:, position]].astype(jnp.float32)
    return running

def one_section(section_args):
    hidden_a, expert_ids_a, router_probs_a, hidden_b, expert_ids_b, router_probs_b, grad_out_b, gain_row, w_gate, w_up, w_down = section_args
    blocks = N_EXPERT

    def block_view(values):
        return values.reshape((blocks, TOK_DEV) + values.shape[1:])

    def prepare(hidden, expert_ids, router_probs):
        normed = normed_rows(hidden, gain_row).astype(jnp.bfloat16)
        weight = router_probs / lax.optimization_barrier(jnp.sum(router_probs, axis=-1, keepdims=True))
        inside, target = route_table(expert_ids, WIN_EXP, CAP)
        sources = slot_sources(target, WIN_EXP, CAP)
        return (normed, weight, inside, target, sources)

    def to_experts(values):
        return jnp.swapaxes(values, 0, 1).reshape(WIN_EXP, blocks * CAP, D)

    def from_experts(values):
        return jnp.swapaxes(values.reshape(WIN_EXP, blocks, CAP, D), 0, 1)
    normed_a, weight_a, inside_a, target_a, sources_a = jax.vmap(prepare)(block_view(hidden_a), block_view(expert_ids_a), block_view(router_probs_a))
    rows_a = jax.vmap(lambda normed, sources: dispatch_rows(normed, sources, TOP, WIN_EXP))(normed_a, sources_a)
    out_a = lax.map(lambda packed: expert_forward(*packed), (to_experts(rows_a), w_gate, w_up, w_down))
    output_a = jax.vmap(combine_rows)(block_view(hidden_a).astype(jnp.float32), weight_a, inside_a, target_a, from_experts(out_a))
    normed_b, weight_b, inside_b, target_b, sources_b = jax.vmap(prepare)(block_view(hidden_b), block_view(expert_ids_b), block_view(router_probs_b))
    rows_b = jax.vmap(lambda normed, sources: dispatch_rows(normed, sources, TOP, WIN_EXP))(normed_b, sources_b)
    scaled_b = jax.vmap(lambda gradients, weight, sources: scaled_rows(gradients, weight, sources, WIN_EXP))(block_view(grad_out_b), weight_b, sources_b)
    back_b = lax.map(lambda packed: expert_backward(*packed), (to_experts(rows_b), to_experts(scaled_b), w_gate, w_up, w_down))
    d_normed = jax.vmap(combine_rows)(jnp.zeros((blocks, TOK_DEV, D), jnp.float32), jnp.ones_like(weight_b), inside_b, target_b, from_experts(back_b))
    _, pullback = jax.vjp(lambda values: normed_rows(values, gain_row), hidden_b.astype(jnp.float32))
    input_grad = grad_out_b.astype(jnp.float32) + pullback(d_normed.reshape(TOKENS, D))[0]
    return (output_a.reshape(TOKENS, D).astype(jnp.bfloat16), input_grad.astype(jnp.bfloat16))

def reference(hidden_a, expert_ids_a, router_probs_a, hidden_b, expert_ids_b, router_probs_b, grad_out_b, norm_gain, w_gate, w_up, w_down):
    output_a, input_grad = lax.map(one_section, (hidden_a, expert_ids_a, router_probs_a, hidden_b, expert_ids_b, router_probs_b, grad_out_b, norm_gain, w_gate, w_up, w_down))
    zero_section = jnp.zeros((1, TOKENS, D), jnp.bfloat16)
    next_hidden_a = jnp.concatenate([zero_section, output_a[:-1]], axis=0)
    grad_in_b = jnp.concatenate([input_grad[1:], zero_section], axis=0)
    return (next_hidden_a, grad_in_b)
```

```python
import jax
import jax.numpy as jnp
from jax import lax
from jax.experimental import pallas as pl
from jax.experimental.pallas import tpu as pltpu
from jax.sharding import PartitionSpec as P

NORM_EPS = 1e-06
MESH = pl.DeviceIdType.MESH
BF = jnp.bfloat16
F32 = jnp.float32
RING = 8
ORDER = (4, 3, 5, 2, 6, 1, 7, 0)
PLACE = {k: s for s, k in enumerate(ORDER)}
GROUPS = ((0, 1), (1, 3), (3, 5), (5, 8))
TILE = 256

ARRIVALS = (
    ((4, 1), (3, 1), (5, 1), (2, 1), (6, 1), "L1", "S1", (1, 1), (7, 1)),
    ((4, 2), (3, 2), (5, 2), (2, 2), (6, 2), "L2", "S2"),
    ((4, 3), (3, 3), (5, 3), "L3", "S3"),
    ((4, 4), "L4"),
)


def hops_of(k):
    return k if k <= 4 else RING - k


HOPS = [(k, h) for k in range(1, RING) for h in range(1, hops_of(k) + 1)]
SLOT = {kh: i for i, kh in enumerate(HOPS)}


def last_dot(left, right):
    return lax.dot_general(left, right, (((1,), (1,)), ((), ())), preferred_element_type=F32)


def dot(left, right):
    return jnp.dot(left, right, preferred_element_type=F32)


def kernel(
    ids_ref, probs_a, probs_b, hid_a, hid_b, grad_b, gain_ref, wg_hbm, wu_hbm, wd_hbm,
    next_ref, prev_ref,
    wg, wu, wd, nn, gg, dd_a, dd_b, ddt_a, ddt_b, hot_a, hot_b,
    send1_a, send1_b, one_a, one_b, esend_a, esend_b,
    ring_a, ring_b, emine_a, emine_b, epart_a, epart_b,
    x_a, x_b, s_b, hid1, hid2, out_a, out_b, back_a, back_b, epin_a, epin_b,
    chain_a, chain_b, etot_a, etot_b, ein_a, ein_b, fin_a, fin_b,
    ret, dnorm, pipe_a, pipe_b, send_sems, recv_sems, local_sems,
):
    pipe = lax.axis_index("pipe")
    pipes = lax.axis_size("pipe")
    me = lax.axis_index("expert")
    core = lax.rem(me, 2)
    z = lax.rem(lax.div(me, 2), RING)
    x = lax.div(me, 2 * RING)
    sg = 1 - 2 * core
    width = hid_a.shape[1]
    half = width // 2
    ff = wg.shape[1]
    tokens = hid_a.shape[0]

    def device(xx, zz, cc):
        return {"expert": (xx * RING + zz) * 2 + cc}

    partner = [
        device(x if q < 2 else 1 - x, z, core if q % 2 == 0 else 1 - core) for q in range(4)
    ]
    long_way = device(x, lax.rem(z + sg + RING, RING), core)
    short_way = device(x, lax.rem(z - sg + RING, RING), core)
    pipe_next = {"pipe": lax.rem(pipe + 1, pipes)}
    pipe_prev = {"pipe": lax.rem(pipe + pipes - 1, pipes)}

    used = [0]
    sent = []

    def describe(src, dst, target):
        i = used[0]
        used[0] += 1
        return pltpu.make_async_remote_copy(
            src_ref=src, dst_ref=dst, send_sem=send_sems.at[i], recv_sem=recv_sems.at[i],
            device_id=target, device_id_type=MESH,
        )

    def send(src, dst, target):
        copy = describe(src, dst, target)
        copy.start()
        sent.append(copy)
        return copy

    weights = []
    for i, (src, dst) in enumerate(((wg_hbm, wg), (wu_hbm, wu), (wd_hbm, wd))):
        copy = pltpu.make_async_copy(src, dst, local_sems.at[i])
        copy.start()
        weights.append(copy)

    barrier = pltpu.get_barrier_semaphore()
    greeted = [partner[1], partner[2], partner[3], long_way, short_way]
    if pipes > 1:
        greeted += [pipe_next, pipe_prev]
    for other in greeted:
        pl.semaphore_signal(barrier, inc=1, device_id=other, device_id_type=MESH)

    def routing(which, dd, ddt, hot):
        ids = ids_ref[which]
        j = lax.broadcasted_iota(jnp.int32, (32, tokens), 0)
        q = j & 3
        s = j >> 2
        k = jnp.where((s & 1) == 1, 3 - (s >> 1), 4 + (s >> 1))
        cq = (core + (q & 1)) & 1
        xq = (x + (q >> 1)) & 1
        zq = (z + (1 - 2 * cq) * k + RING) & (RING - 1)
        expert = (xq * RING + zq) * 2 + cq
        match = (ids[0:1, :] == expert) | (ids[1:2, :] == expert)
        matched = jnp.where(match, 1.0, 0.0)
        t0 = lax.broadcasted_iota(jnp.int32, (tokens, tokens), 0)
        t1 = lax.broadcasted_iota(jnp.int32, (tokens, tokens), 1)
        rank = dot(matched.astype(BF), jnp.where(t0 < t1, 1.0, 0.0).astype(BF))
        ranked = jnp.where(match, rank, 200.0)
        own = q < 2
        rank_own = jnp.sum(jnp.where(own, matched * rank, 0.0), axis=0, keepdims=True)
        rank_other = jnp.sum(jnp.where(own, 0.0, matched * rank), axis=0, keepdims=True)
        hot[...] = dot(matched.astype(BF), jnp.ones((tokens, TILE), BF))
        r = lax.broadcasted_iota(jnp.int32, (256, 32), 0)
        cols = lax.broadcasted_iota(jnp.int32, (256, 32), 1)
        spread = jnp.where((r >> 3) == cols, 1.0, 0.0).astype(BF)
        rows = dot(spread, ranked.astype(BF))
        r = lax.broadcasted_iota(jnp.int32, (256, tokens), 0)
        hit = rows == (r & 7).astype(F32)
        mine = ((r >> 3) & 3) < 2
        dd[0:256, 0:tokens] = jnp.where(hit & mine, 1.0, 0.0).astype(BF)
        dd[0:256, tokens:] = jnp.where(hit & jnp.logical_not(mine), 1.0, 0.0).astype(BF)
        r = lax.broadcasted_iota(jnp.int32, (128, tokens), 0)
        rf = r.astype(F32)
        dd[256:384, 0:tokens] = jnp.where((rank_own == rf + 8.0) & (r < 8), 1.0, 0.0).astype(BF)
        dd[256:384, tokens:] = jnp.where(
            (rank_other == rf) & (r >= 8) & (r < 16), 1.0, 0.0
        ).astype(BF)
        t0 = lax.broadcasted_iota(jnp.int32, (2 * tokens, 2 * tokens), 0)
        t1 = lax.broadcasted_iota(jnp.int32, (2 * tokens, 2 * tokens), 1)
        eye = jnp.where(t0 == t1, 1.0, 0.0).astype(BF)
        ddt[...] = last_dot(eye, dd[...]).astype(BF)

    xf = x.astype(F32)

    def gates(probs):
        weight = probs / jnp.sum(probs, axis=-1, keepdims=True)
        first, second = weight[:, 0:1], weight[:, 1:2]
        return first * (1.0 - xf) + second * xf, second * (1.0 - xf) + first * xf

    def inverse_norm(values):
        return lax.rsqrt(jnp.mean(values * values, axis=-1, keepdims=True) + NORM_EPS)

    def prepare(hidden, probs, gradient):
        @pl.loop(0, tokens // 16)
        def _(i):
            rows = pl.ds(pl.multiple_of(i * 16, 16), 16)
            later = pl.ds(pl.multiple_of(tokens + i * 16, 16), 16)
            values = hidden[rows, :].astype(F32)
            normed = (values * inverse_norm(values) * gain_ref[...]).astype(BF)
            nn[rows, :] = normed
            nn[later, :] = normed
            if gradient is not None:
                own, other = gates(probs[rows, :])
                up = gradient[rows, :].astype(F32)
                gg[rows, :] = (own * up).astype(BF)
                gg[later, :] = (other * up).astype(BF)

    def pack(dd, send1, one, emine, esend, first, second, wide):
        step = min(512, wide)

        @pl.loop(0, wide // step)
        def _(i):
            cols = pl.ds(pl.multiple_of(i * step, step), step)
            top = dot(dd[0:272, :], first(i * step, step))
            low = dot(dd[0:272, :], second(i * step, step))
            both = jnp.concatenate(
                [top.reshape(34, 8, step), low.reshape(34, 8, step)], axis=1
            ).astype(BF)
            blocks = both[0:32].reshape(8, 4, 16, step)
            one[:, 0, :, cols] = blocks[:, 0]
            send1[:, :, :, cols] = blocks[:, 1:4]
            emine[0, 0, :, cols] = both[32]
            esend[:, cols] = both[33]

    def columns(ref, base):
        def take(start, size):
            return ref[:, pl.ds(pl.multiple_of(base + start, size), size)]

        return take

    class Dispatch:
        def __init__(self, send1, one, esend, emine, epart, ring, unpack):
            self.send1, self.one, self.esend, self.emine = send1, one, esend, emine
            self.epart, self.ring, self.unpack = epart, ring, unpack
            self.hop = {}
            self.part = {}

        def exchange(self):
            self.first = []
            self.e_first = None
            for n, (a, b) in enumerate(GROUPS):
                at = pl.ds(a, b - a)
                self.first.append([
                    send(self.send1.at[at, q - 1], self.one.at[at, q], partner[q])
                    for q in (1, 2, 3)
                ])
                if n == 2:
                    self.e_first = send(self.esend, self.emine.at[0, 1], partner[2])

        def forward(self, k, h):
            src = self.one.at[PLACE[k]] if h == 1 else self.ring.at[SLOT[k, h - 1]]
            target = long_way if k <= 4 else short_way
            self.hop[k, h] = send(src, self.ring.at[SLOT[k, h]], target)

        def forward_extra(self, way, h):
            if way == "L":
                copy = send(self.emine.at[h - 1], self.emine.at[h], long_way)
            else:
                copy = send(self.emine.at[(9 - h) % 8], self.emine.at[8 - h], short_way)
            self.hop[way, h] = copy

        def swap_extra(self, k):
            self.part[k] = send(self.emine.at[k], self.epart.at[k], partner[1])

        def launch(self, group):
            for copy in self.first[group]:
                copy.wait_recv()
            for s in range(*GROUPS[group]):
                if ORDER[s]:
                    self.forward(ORDER[s], 1)
            if group == 2:
                self.e_first.wait_recv()
                self.forward_extra("L", 1)
                self.forward_extra("S", 1)
                self.swap_extra(0)

        def local(self):
            self.unpack(self.one.at[PLACE[0]], 0)
            self.unpack(self.emine.at[0], 256)

        def arrive(self, event):
            if isinstance(event, str):
                way, h = event[0], int(event[1])
                self.hop[way, h].wait_recv()
                if h < (4 if way == "L" else 3):
                    self.forward_extra(way, h + 1)
                k = h if way == "L" else 8 - h
                self.swap_extra(k)
                self.unpack(self.emine.at[k], 256 + k * 16)
            else:
                k, h = event
                self.hop[k, h].wait_recv()
                if h < hops_of(k):
                    self.forward(k, h + 1)
                else:
                    self.unpack(self.ring.at[SLOT[k, h]], k * 32)

        def finish(self):
            for k in (0, 1, 7, 2, 6, 3, 5, 4):
                self.part[k].wait_recv()
                self.unpack(self.epart.at[k], 384 + k * 16)

    def unpack_b(src, row):
        count = src.shape[0]
        values = src[...].astype(F32).reshape(count, 2, 8, width)
        rows = pl.ds(row, count * 8)
        x_b[rows, :] = values[:, 0].reshape(count * 8, width).astype(BF)
        s_b[rows, :] = values[:, 1].reshape(count * 8, width).astype(BF)

    def unpack_a(src, row):
        count = src.shape[0]
        values = src[...].astype(F32).reshape(count, 2, 8, half)
        rows = pl.ds(row, count * 8)
        x_a[rows, 0:half] = values[:, 0].reshape(count * 8, half).astype(BF)
        x_a[rows, half:] = values[:, 1].reshape(count * 8, half).astype(BF)

    def tile_at(i):
        return pl.ds(pl.multiple_of(i * TILE, TILE), TILE)

    def forward_units(i):
        cols = tile_at(i)
        gate_pre = dot(x_a[...], wg[:, cols])
        up_pre = dot(x_a[...], wu[:, cols])
        hid1[:, cols] = (gate_pre * jax.nn.sigmoid(gate_pre) * up_pre).astype(BF)

    def backward_units(i):
        cols = tile_at(i)
        gate_pre = dot(x_b[...], wg[:, cols])
        up_pre = dot(x_b[...], wu[:, cols])
        d_hidden = last_dot(s_b[...], wd[cols, :])
        sigma = jax.nn.sigmoid(gate_pre)
        hid1[:, cols] = (d_hidden * up_pre * sigma * (1.0 + gate_pre * (1.0 - sigma))).astype(BF)
        hid2[:, cols] = (d_hidden * gate_pre * sigma).astype(BF)

    def store_out(out, hot, i, low, high):
        valid = jnp.broadcast_to(hot[28:29, :], (256, TILE)) > 8.5
        both = []
        for part in (low, high):
            extra = jnp.where(valid, part[256:512], 0.0)
            both.append(jnp.concatenate([part[0:256], extra], axis=0).reshape(64, 8, TILE))
        out[:, :, tile_at(i)] = jnp.concatenate(both, axis=1).astype(BF)

    def forward_out(i):
        low = dot(hid1[...], wd[:, tile_at(i)])
        high = dot(hid1[...], wd[:, pl.ds(pl.multiple_of(half + i * TILE, TILE), TILE)])
        store_out(out_a, hot_a, i, low, high)

    def backward_out(i):
        later = pl.ds(pl.multiple_of(half + i * TILE, TILE), TILE)
        low = last_dot(hid1[...], wg[tile_at(i), :]) + last_dot(hid2[...], wu[tile_at(i), :])
        high = last_dot(hid1[...], wg[later, :]) + last_dot(hid2[...], wu[later, :])
        store_out(out_b, hot_b, i, low, high)

    def run(step, first, last):
        @pl.loop(first, last)
        def _(i):
            step(i)

    class Return:
        def __init__(self, out, back, epin, chain, etot, ein, fin):
            self.out, self.back, self.epin, self.chain = out, back, epin, chain
            self.etot, self.ein, self.fin = etot, ein, fin
            self.hop = {}
            self.last = []

        def swap(self):
            self.swapped = send(self.out.at[pl.ds(48, 16)], self.epin, partner[1])

        def forward(self, k, h):
            src = self.out.at[pl.ds(4 * k, 4)] if h == 1 else self.back.at[SLOT[k, h - 1]]
            target = short_way if k <= 4 else long_way
            self.hop[k, h] = send(src, self.back.at[SLOT[k, h]], target)

        def launch(self):
            self.swap()
            for s in range(7):
                self.forward(ORDER[s], 1)

        def launch_extra(self):
            self.swapped.wait_recv()
            self.epin[...] = (self.out[32:48].astype(F32) + self.epin[...].astype(F32)).astype(BF)
            self.hop["L", 1] = send(self.epin.at[pl.ds(8, 2)], self.chain.at[0], short_way)
            self.hop["S", 1] = send(self.epin.at[pl.ds(10, 2)], self.chain.at[4], long_way)

        def distribute(self, k):
            src = self.out.at[pl.ds(0, 4)] if k == 0 else self.back.at[SLOT[k, hops_of(k)]]
            for q in (2, 3, 1):
                self.last.append(send(src.at[q], self.fin.at[k, q - 1], partner[q]))

        def arrive(self, event):
            if isinstance(event, str):
                way, h = event[0], int(event[1])
                self.hop[way, h].wait_recv()
                k = 4 - h if way == "L" else 5 + h
                at = h - 1 if way == "L" else 3 + h
                if h < (4 if way == "L" else 3):
                    mine = self.epin[2 * k:2 * k + 2].astype(F32)
                    self.chain[at] = (self.chain[at].astype(F32) + mine).astype(BF)
                    target = short_way if way == "L" else long_way
                    self.hop[way, h + 1] = send(
                        self.chain.at[at], self.chain.at[at + 1], target
                    )
            else:
                k, h = event
                self.hop[k, h].wait_recv()
                if h < hops_of(k):
                    self.forward(k, h + 1)
                else:
                    self.distribute(k)

        def finish_extra(self):
            total = self.epin[0:2].astype(F32) + self.chain[3].astype(F32)
            self.etot[...] = (total + self.chain[6].astype(F32)).astype(BF)
            self.last.append(send(self.etot.at[1], self.ein, partner[2]))

        def collect(self):
            for copy in self.last:
                copy.wait_recv()
            for k in range(RING):
                own = self.out[0:1] if k == 0 else self.back[SLOT[k, hops_of(k)], 0:1]
                block = jnp.concatenate([own.astype(F32), self.fin[k].astype(F32)], axis=0)
                block = block.reshape(4, 2, 8, half)
                at = PLACE[k] * 32
                ret[at:at + 32, 0:half] = block[:, 0].reshape(32, half).astype(BF)
                ret[at:at + 32, half:] = block[:, 1].reshape(32, half).astype(BF)
            own, other = self.etot[0].astype(F32), self.ein[...].astype(F32)
            ret[256:272, 0:half] = jnp.concatenate([own[0:8], other[0:8]], axis=0).astype(BF)
            ret[256:272, half:] = jnp.concatenate([own[8:16], other[8:16]], axis=0).astype(BF)

    dis_a = Dispatch(send1_a, one_a, esend_a, emine_a, epart_a, ring_a, unpack_a)
    dis_b = Dispatch(send1_b, one_b, esend_b, emine_b, epart_b, ring_b, unpack_b)
    ret_a = Return(out_a, back_a, epin_a, chain_a, etot_a, ein_a, fin_a)
    ret_b = Return(out_b, back_b, epin_b, chain_b, etot_b, ein_b, fin_b)

    routing(1, dd_b, ddt_b, hot_b)
    prepare(hid_b, probs_b, grad_b)
    pack(dd_b, send1_b, one_b, emine_b, esend_b, columns(nn, 0), columns(gg, 0), width)
    pl.semaphore_wait(barrier, len(greeted))
    dis_b.exchange()

    routing(0, dd_a, ddt_a, hot_a)
    prepare(hid_a, probs_a, None)
    pack(dd_a, send1_a, one_a, emine_a, esend_a, columns(nn, 0), columns(nn, half), half)
    ret[272:384, :] = jnp.zeros((112, width), BF)

    for group in range(4):
        dis_b.launch(group)
    dis_a.exchange()
    dis_b.local()
    for event in ARRIVALS[0] + ARRIVALS[1]:
        dis_b.arrive(event)
    for group in range(4):
        dis_a.launch(group)
    dis_a.local()
    for event in ARRIVALS[2] + ARRIVALS[3]:
        dis_b.arrive(event)
    dis_b.finish()
    for copy in weights:
        copy.wait()

    tiles = ff // TILE
    for event in ARRIVALS[0]:
        dis_a.arrive(event)
    run(backward_units, 0, tiles)
    for event in ARRIVALS[1]:
        dis_a.arrive(event)
    outs = half // TILE
    run(backward_out, 0, outs)
    ret_b.launch()
    for event in ARRIVALS[2] + ARRIVALS[3]:
        dis_a.arrive(event)
    ret_b.launch_extra()
    ret_b.distribute(0)
    dis_a.finish()
    for event in ARRIVALS[0]:
        ret_b.arrive(event)
    run(forward_units, 0, tiles)
    for event in ARRIVALS[1]:
        ret_b.arrive(event)
    run(forward_out, 0, outs)
    ret_a.launch()
    for event in ARRIVALS[2] + ARRIVALS[3]:
        ret_b.arrive(event)
    ret_b.finish_extra()
    ret_a.launch_extra()
    ret_a.distribute(0)
    for event in ARRIVALS[0]:
        ret_a.arrive(event)
    ret_b.collect()

    step = min(512, width)

    @pl.loop(0, width // step)
    def _(i):
        cols = pl.ds(pl.multiple_of(i * step, step), step)
        moved = dot(ddt_b[...], ret[:, cols])
        dnorm[:, cols] = moved[0:tokens] + moved[tokens:]

    @pl.loop(0, tokens // 16)
    def _(i):
        rows = pl.ds(pl.multiple_of(i * 16, 16), 16)
        values = hid_b[rows, :].astype(F32)
        r = inverse_norm(values)
        scaled = dnorm[rows, :] * gain_ref[...]
        inner = jnp.mean(values * scaled, axis=-1, keepdims=True)
        grown = grad_b[rows, :].astype(F32) + r * scaled - values * (r * r * r * inner)
        pipe_b[rows, :] = grown.astype(BF)

    to_prev = describe(pipe_b, prev_ref, pipe_prev)
    if pipes > 1:
        @pl.when(pipe > 0)
        def _():
            to_prev.start()

    for event in ARRIVALS[1] + ARRIVALS[2] + ARRIVALS[3]:
        ret_a.arrive(event)
    ret_a.finish_extra()
    ret_a.collect()

    own_gate, other_gate = gates(probs_a[...])

    @pl.loop(0, width // step)
    def _(i):
        cols = pl.ds(pl.multiple_of(i * step, step), step)
        moved = dot(ddt_a[...], ret[:, cols])
        summed = own_gate * moved[0:tokens] + other_gate * moved[tokens:]
        pipe_a[:, cols] = (hid_a[:, cols].astype(F32) + summed).astype(BF)

    to_next = describe(pipe_a, next_ref, pipe_next)
    if pipes > 1:
        @pl.when(pipe < pipes - 1)
        def _():
            to_next.start()

    @pl.when(pipe == 0)
    def _():
        next_ref[...] = jnp.zeros(next_ref.shape, BF)

    @pl.when(pipe == pipes - 1)
    def _():
        prev_ref[...] = jnp.zeros(prev_ref.shape, BF)

    for copy in sent:
        copy.wait_send()
    if pipes > 1:
        @pl.when(pipe < pipes - 1)
        def _():
            to_prev.wait_recv()
            to_next.wait_send()

        @pl.when(pipe > 0)
        def _():
            to_next.wait_recv()
            to_prev.wait_send()


def scratch(tokens, width, ff):
    half = width // 2
    vmem = pltpu.VMEM
    hops = len(HOPS)
    shapes = [
        ((width, ff), BF), ((width, ff), BF), ((ff, width), BF),
        ((2 * tokens, width), BF), ((2 * tokens, width), BF),
        ((384, 2 * tokens), BF), ((384, 2 * tokens), BF),
        ((2 * tokens, 384), BF), ((2 * tokens, 384), BF),
        ((32, TILE), F32), ((32, TILE), F32),
        ((8, 3, 16, half), BF), ((8, 3, 16, width), BF),
        ((8, 4, 16, half), BF), ((8, 4, 16, width), BF),
        ((16, half), BF), ((16, width), BF),
        ((hops, 4, 16, half), BF), ((hops, 4, 16, width), BF),
        ((8, 2, 16, half), BF), ((8, 2, 16, width), BF),
        ((8, 2, 16, half), BF), ((8, 2, 16, width), BF),
        ((512, width), BF), ((512, width), BF), ((512, width), BF),
        ((512, ff), BF), ((512, ff), BF),
        ((64, 16, half), BF), ((64, 16, half), BF),
        ((hops, 4, 16, half), BF), ((hops, 4, 16, half), BF),
        ((16, 16, half), BF), ((16, 16, half), BF),
        ((7, 2, 16, half), BF), ((7, 2, 16, half), BF),
        ((2, 16, half), BF), ((2, 16, half), BF),
        ((16, half), BF), ((16, half), BF),
        ((8, 3, 16, half), BF), ((8, 3, 16, half), BF),
        ((384, width), BF), ((tokens, width), F32),
        ((tokens, width), BF), ((tokens, width), BF),
    ]
    messages = 256
    return [vmem(shape, kind) for shape, kind in shapes] + [
        pltpu.SemaphoreType.DMA((messages,)),
        pltpu.SemaphoreType.DMA((messages,)),
        pltpu.SemaphoreType.DMA((3,)),
    ]


def per_device(
    hidden_a, expert_ids_a, router_probs_a, hidden_b, expert_ids_b, router_probs_b,
    grad_out_b, norm_gain, w_gate, w_up, w_down,
):
    tokens, width = hidden_a.shape[1:]
    ff = w_gate.shape[3]
    ids = jnp.swapaxes(jnp.concatenate([expert_ids_a, expert_ids_b], axis=0), 1, 2)
    inside = pl.BlockSpec(memory_space=pltpu.VMEM)
    outside = pl.BlockSpec(memory_space=pl.ANY)
    result = jax.ShapeDtypeStruct((tokens, width), BF)
    rows = 512
    next_hidden, grad_before = pl.pallas_call(
        kernel,
        out_shape=(result, result),
        in_specs=[inside] * 7 + [outside] * 3,
        out_specs=(inside, inside),
        scratch_shapes=scratch(tokens, width, ff),
        compiler_params=pltpu.CompilerParams(
            collective_id=0, has_side_effects=True, vmem_limit_bytes=60 * 1024 * 1024
        ),
        cost_estimate=pl.CostEstimate(
            flops=2 * rows * width * ff * 8, bytes_accessed=6 * width * ff, transcendentals=0
        ),
    )(
        ids, router_probs_a[0], router_probs_b[0], hidden_a[0], hidden_b[0], grad_out_b[0],
        norm_gain, w_gate[0, 0], w_up[0, 0], w_down[0, 0],
    )
    return next_hidden[None], grad_before[None]


def solution(mesh):
    in_specs = (
        P("pipe", "expert", None),
        P("pipe", "expert", None),
        P("pipe", "expert", None),
        P("pipe", "expert", None),
        P("pipe", "expert", None),
        P("pipe", "expert", None),
        P("pipe", "expert", None),
        P("pipe", None),
        P("pipe", "expert", None, None),
        P("pipe", "expert", None, None),
        P("pipe", "expert", None, None),
    )
    out_specs = (P("pipe", "expert", None), P("pipe", "expert", None))
    return jax.shard_map(
        per_device, mesh=mesh, in_specs=in_specs, out_specs=out_specs, check_vma=False
    )
```

```python
import jax
import jax.numpy as jnp
from jax import lax
from jax.experimental import pallas as pl
from jax.experimental.pallas import tpu as pltpu
from jax.sharding import PartitionSpec as P

NORM_EPS = 1e-06
MESH = pl.DeviceIdType.MESH
BF = jnp.bfloat16
F32 = jnp.float32
RING = 8
ORDER = (4, 3, 5, 2, 6, 1, 7, 0)
PLACE = {k: s for s, k in enumerate(ORDER)}
TILE = 256
PARTS_A = 2
BLOCKS = [(k, q) for k in ORDER for q in (2, 3, 0, 1) if (k, q) != (0, 0)]
EXTRA_HOPS = {"L": 4, "S": 3}


def chunks(count):
    size = -(-len(BLOCKS) // count)
    return [BLOCKS[i:i + size] for i in range(0, len(BLOCKS), size)]


def last_dot(left, right):
    return lax.dot_general(left, right, (((1,), (1,)), ((), ())), preferred_element_type=F32)


def dot(left, right):
    return jnp.dot(left, right, preferred_element_type=F32)


def kernel(
    ids_ref, probs_ref, hid_a, hid_b, grad_b, gain_ref, wg_hbm, wu_hbm, wd_hbm,
    next_ref, prev_ref,
    wg, wu, wd, nn, gg, dd_a, dd_b, ddt_a, ddt_b, hot_a, hot_b, gates_a, gates_b,
    send1_a, send1_b, rx_a, rx_b, esend_a, esend_b, emine_a, emine_b, epart_a, epart_b,
    x_a, x_b, s_b, hid1, hid2, out_a, out_b, epin_a, epin_b,
    chain_a, chain_b, etot_a, etot_b, ein_a, ein_b, fin_a, fin_b,
    ret, dnorm, pipe_a, pipe_b, send_sems, recv_sems, local_sems,
):
    pipe = lax.axis_index("pipe")
    pipes = lax.axis_size("pipe")
    me = lax.axis_index("expert")
    core = lax.rem(me, 2)
    z = lax.rem(lax.div(me, 2), RING)
    x = lax.div(me, 2 * RING)
    sg = 1 - 2 * core
    width = hid_a.shape[1]
    half = width // 2
    ff = wg.shape[1]
    tokens = hid_a.shape[0]

    def device(xx, zz, cc):
        return {"expert": (xx * RING + zz) * 2 + cc}

    partner = [
        device(x if q < 2 else 1 - x, z, core if q % 2 == 0 else 1 - core) for q in range(4)
    ]

    def target(k, q):
        cc = core if q % 2 == 0 else 1 - core
        return device(x if q < 2 else 1 - x, lax.rem(z + (1 - 2 * cc) * k + RING, RING), cc)

    def source(k, q):
        cc = core if q % 2 == 0 else 1 - core
        return device(x if q < 2 else 1 - x, lax.rem(z - sg * k + RING, RING), cc)

    long_way = device(x, lax.rem(z + sg + RING, RING), core)
    short_way = device(x, lax.rem(z - sg + RING, RING), core)
    pipe_next = {"pipe": lax.rem(pipe + 1, pipes)}
    pipe_prev = {"pipe": lax.rem(pipe + pipes - 1, pipes)}

    used = [0]
    sent = []

    def describe(src, dst, target):
        i = used[0]
        used[0] += 1
        return pltpu.make_async_remote_copy(
            src_ref=src, dst_ref=dst, send_sem=send_sems.at[i], recv_sem=recv_sems.at[i],
            device_id=target, device_id_type=MESH,
        )

    def send(src, dst, target):
        copy = describe(src, dst, target)
        copy.start()
        sent.append(copy)
        return copy

    weights = []
    for i, (src, dst) in enumerate(((wg_hbm, wg), (wu_hbm, wu), (wd_hbm, wd))):
        copy = pltpu.make_async_copy(src, dst, local_sems.at[i])
        copy.start()
        weights.append(copy)

    barrier = pltpu.get_barrier_semaphore()
    greeted = [target(k, q) for k, q in BLOCKS]
    if pipes > 1:
        greeted += [pipe_next, pipe_prev]
    for other in greeted:
        pl.semaphore_signal(barrier, inc=1, device_id=other, device_id_type=MESH)

    def routing(which, dd, ddt, hot):
        ids = ids_ref[which]
        j = lax.broadcasted_iota(jnp.int32, (32, tokens), 0)
        q = j & 3
        s = j >> 2
        k = jnp.where((s & 1) == 1, 3 - (s >> 1), 4 + (s >> 1))
        cq = (core + (q & 1)) & 1
        xq = (x + (q >> 1)) & 1
        zq = (z + (1 - 2 * cq) * k + RING) & (RING - 1)
        expert = (xq * RING + zq) * 2 + cq
        match = (ids[0:1, :] == expert) | (ids[1:2, :] == expert)
        matched = jnp.where(match, 1.0, 0.0)
        t0 = lax.broadcasted_iota(jnp.int32, (tokens, tokens), 0)
        t1 = lax.broadcasted_iota(jnp.int32, (tokens, tokens), 1)
        rank = dot(matched.astype(BF), jnp.where(t0 < t1, 1.0, 0.0).astype(BF))
        ranked = jnp.where(match, rank, 200.0)
        own = q < 2
        rank_own = jnp.sum(jnp.where(own, matched * rank, 0.0), axis=0, keepdims=True)
        rank_other = jnp.sum(jnp.where(own, 0.0, matched * rank), axis=0, keepdims=True)
        hot[...] = dot(matched.astype(BF), jnp.ones((tokens, TILE), BF))
        r = lax.broadcasted_iota(jnp.int32, (256, 32), 0)
        cols = lax.broadcasted_iota(jnp.int32, (256, 32), 1)
        spread = jnp.where((r >> 3) == cols, 1.0, 0.0).astype(BF)
        rows = dot(spread, ranked.astype(BF))
        r = lax.broadcasted_iota(jnp.int32, (256, tokens), 0)
        hit = rows == (r & 7).astype(F32)
        mine = ((r >> 3) & 3) < 2
        dd[0:256, 0:tokens] = jnp.where(hit & mine, 1.0, 0.0).astype(BF)
        dd[0:256, tokens:] = jnp.where(hit & jnp.logical_not(mine), 1.0, 0.0).astype(BF)
        r = lax.broadcasted_iota(jnp.int32, (128, tokens), 0)
        rf = r.astype(F32)
        dd[256:384, 0:tokens] = jnp.where((rank_own == rf + 8.0) & (r < 8), 1.0, 0.0).astype(BF)
        dd[256:384, tokens:] = jnp.where(
            (rank_other == rf) & (r >= 8) & (r < 16), 1.0, 0.0
        ).astype(BF)
        t0 = lax.broadcasted_iota(jnp.int32, (2 * tokens, 2 * tokens), 0)
        t1 = lax.broadcasted_iota(jnp.int32, (2 * tokens, 2 * tokens), 1)
        eye = jnp.where(t0 == t1, 1.0, 0.0).astype(BF)
        ddt[...] = last_dot(eye, dd[...]).astype(BF)

    xf = x.astype(F32)

    def gates(which, gate):
        probs = probs_ref[which]
        weight = probs / jnp.sum(probs, axis=0, keepdims=True)
        first, second = weight[0:1, :], weight[1:2, :]
        for i, row in enumerate(
            (first * (1.0 - xf) + second * xf, second * (1.0 - xf) + first * xf)
        ):
            gate[i] = jnp.broadcast_to(row, (tokens, tokens)).T

    def inverse_norm(values):
        return lax.rsqrt(jnp.mean(values * values, axis=-1, keepdims=True) + NORM_EPS)

    def prepare(hidden, gate, gradient):
        @pl.loop(0, tokens // 16)
        def _(i):
            rows = pl.ds(pl.multiple_of(i * 16, 16), 16)
            later = pl.ds(pl.multiple_of(tokens + i * 16, 16), 16)
            values = hidden[rows, :].astype(F32)
            normed = (values * inverse_norm(values) * gain_ref[...]).astype(BF)
            nn[rows, :] = normed
            nn[later, :] = normed
            if gradient is not None:
                up = gradient[rows, :].astype(F32)
                gg[rows, :] = (gate[0, rows, 0:1] * up).astype(BF)
                gg[later, :] = (gate[1, rows, 0:1] * up).astype(BF)

    def pack(dd, send1, rx, emine, esend, first, second, wide):
        step = min(512, wide)

        @pl.loop(0, wide // step)
        def _(i):
            cols = pl.ds(pl.multiple_of(i * step, step), step)
            top = dot(dd[0:272, :], first(i * step, step))
            low = dot(dd[0:272, :], second(i * step, step))
            both = jnp.concatenate(
                [top.reshape(34, 8, step), low.reshape(34, 8, step)], axis=1
            ).astype(BF)
            send1[:, :, :, cols] = both[0:32].reshape(8, 4, 16, step)
            rx[0, 0, :, cols] = both[4 * PLACE[0]]
            emine[0, 0, :, cols] = both[32]
            esend[:, cols] = both[33]

    def columns(ref, base):
        def take(start, size):
            return ref[:, pl.ds(pl.multiple_of(base + start, size), size)]

        return take

    class Dispatch:
        def __init__(self, send1, rx, esend, emine, epart, unpack):
            self.send1, self.rx, self.esend, self.emine = send1, rx, esend, emine
            self.epart, self.unpack = epart, unpack
            self.main, self.hop, self.part = {}, {}, {}

        def launch(self, blocks):
            for k, q in blocks:
                self.main[k, q] = send(
                    self.send1.at[PLACE[k], q], self.rx.at[k, q], target(k, q)
                )

        def start_extra(self):
            self.e_first = send(self.esend, self.emine.at[0, 1], partner[2])

        def swap_extra(self, k):
            self.part[k] = send(self.emine.at[k], self.epart.at[k], partner[1])

        def extra(self, h):
            if h == 1:
                self.e_first.wait_recv()
            for way, last in EXTRA_HOPS.items():
                if 1 < h <= last + 1:
                    self.hop[way, h - 1].wait_recv()
                if h <= last:
                    a, b = (h - 1, h) if way == "L" else ((9 - h) % RING, RING - h)
                    self.hop[way, h] = send(
                        self.emine.at[a], self.emine.at[b],
                        long_way if way == "L" else short_way,
                    )
            if h <= 5:
                for k in {h - 1, (9 - h) % RING} if h <= 4 else {4}:
                    self.swap_extra(k)

        def collect(self):
            for k in ORDER:
                for q in range(4):
                    if (k, q) != (0, 0):
                        self.main[k, q].wait_recv()
                self.unpack(self.rx.at[k], k * 32)
            for k in (0, 1, 7, 2, 6, 3, 5, 4):
                self.unpack(self.emine.at[k], 256 + k * 16)
                self.part[k].wait_recv()
                self.unpack(self.epart.at[k], 384 + k * 16)

    def unpack_b(src, row):
        count = src.shape[0]
        values = src[...].astype(F32).reshape(count, 2, 8, width)
        rows = pl.ds(row, count * 8)
        x_b[rows, :] = values[:, 0].reshape(count * 8, width).astype(BF)
        s_b[rows, :] = values[:, 1].reshape(count * 8, width).astype(BF)

    def unpack_a(src, row):
        count = src.shape[0]
        values = src[...].astype(F32).reshape(count, 2, 8, half)
        rows = pl.ds(row, count * 8)
        x_a[rows, 0:half] = values[:, 0].reshape(count * 8, half).astype(BF)
        x_a[rows, half:] = values[:, 1].reshape(count * 8, half).astype(BF)

    def tile_at(i):
        return pl.ds(pl.multiple_of(i * TILE, TILE), TILE)

    def forward_units(i):
        cols = tile_at(i)
        gate_pre = dot(x_a[...], wg[:, cols])
        up_pre = dot(x_a[...], wu[:, cols])
        hid1[:, cols] = (gate_pre * jax.nn.sigmoid(gate_pre) * up_pre).astype(BF)

    def backward_units(i):
        cols = tile_at(i)
        gate_pre = dot(x_b[...], wg[:, cols])
        up_pre = dot(x_b[...], wu[:, cols])
        d_hidden = last_dot(s_b[...], wd[cols, :])
        sigma = jax.nn.sigmoid(gate_pre)
        hid1[:, cols] = (d_hidden * up_pre * sigma * (1.0 + gate_pre * (1.0 - sigma))).astype(BF)
        hid2[:, cols] = (d_hidden * gate_pre * sigma).astype(BF)

    def store_out(out, part, hot, i, low, high):
        valid = jnp.broadcast_to(hot[28:29, :], (256, TILE)) > 8.5
        both = []
        for half_rows in (low, high):
            extra = jnp.where(valid, half_rows[256:512], 0.0)
            both.append(
                jnp.concatenate([half_rows[0:256], extra], axis=0).reshape(64, 8, TILE)
            )
        out[part, :, :, tile_at(i)] = jnp.concatenate(both, axis=1).astype(BF)

    def shifted(base, i):
        return pl.ds(pl.multiple_of(base + i * TILE, TILE), TILE)

    def forward_out(part):
        wide = out_a.shape[3]

        def step(i):
            low = dot(hid1[...], wd[:, shifted(2 * part * wide, i)])
            high = dot(hid1[...], wd[:, shifted((2 * part + 1) * wide, i)])
            store_out(out_a, part, hot_a, i, low, high)

        return step

    def backward_out(i):
        now, later = shifted(0, i), shifted(half, i)
        low = last_dot(hid1[...], wg[now, :]) + last_dot(hid2[...], wu[now, :])
        high = last_dot(hid1[...], wg[later, :]) + last_dot(hid2[...], wu[later, :])
        store_out(out_b, 0, hot_b, i, low, high)

    def run(step, first, last):
        @pl.loop(first, last)
        def _(i):
            step(i)

    class Return:
        def __init__(self, out, epin, chain, etot, ein, fin):
            self.out, self.epin, self.chain = out, epin, chain
            self.etot, self.ein, self.fin = etot, ein, fin
            self.main, self.hop = {}, {}

        def launch(self, part, blocks):
            for k, q in blocks:
                self.main[part, k, q] = send(
                    self.out.at[part, 4 * k + q], self.fin.at[part, k, q], source(k, q)
                )

        def swap(self):
            self.swapped = send(self.out.at[:, pl.ds(48, 16)], self.epin, partner[1])

        def extra(self, h):
            if h == 1:
                self.swapped.wait_recv()
                mine = self.out[:, 32:48].astype(F32)
                self.epin[...] = (mine + self.epin[...].astype(F32)).astype(BF)
                self.hop["L", 1] = send(
                    self.epin.at[:, pl.ds(8, 2)], self.chain.at[0], short_way
                )
                self.hop["S", 1] = send(
                    self.epin.at[:, pl.ds(10, 2)], self.chain.at[4], long_way
                )
                return
            for way, last in EXTRA_HOPS.items():
                if h > last:
                    continue
                self.hop[way, h - 1].wait_recv()
                k, at = (5 - h, h - 2) if way == "L" else (4 + h, 2 + h)
                mine = self.epin[:, 2 * k:2 * k + 2].astype(F32)
                self.chain[at] = (self.chain[at].astype(F32) + mine).astype(BF)
                self.hop[way, h] = send(
                    self.chain.at[at], self.chain.at[at + 1],
                    short_way if way == "L" else long_way,
                )

        def finish_extra(self):
            self.hop["L", 4].wait_recv()
            self.hop["S", 3].wait_recv()
            total = self.epin[:, 0:2].astype(F32) + self.chain[3].astype(F32)
            self.etot[...] = (total + self.chain[6].astype(F32)).astype(BF)
            self.e_last = send(self.etot.at[:, 1], self.ein, partner[2])

        def collect(self, part):
            wide = self.out.shape[3]
            low = pl.ds(2 * part * wide, wide)
            high = pl.ds((2 * part + 1) * wide, wide)
            for k in ORDER:
                for q in range(4):
                    if (k, q) != (0, 0):
                        self.main[part, k, q].wait_recv()
                block = self.fin[part, k].astype(F32)
                if k == 0:
                    own = self.out[part, 0:1].astype(F32)
                    block = jnp.concatenate([own, block[1:4]], axis=0)
                block = block.reshape(4, 2, 8, wide)
                rows = pl.ds(PLACE[k] * 32, 32)
                ret[rows, low] = block[:, 0].reshape(32, wide).astype(BF)
                ret[rows, high] = block[:, 1].reshape(32, wide).astype(BF)
            if part == 0:
                self.e_last.wait_recv()
            own, other = self.etot[part, 0].astype(F32), self.ein[part].astype(F32)
            ret[256:272, low] = jnp.concatenate([own[0:8], other[0:8]], axis=0).astype(BF)
            ret[256:272, high] = jnp.concatenate([own[8:16], other[8:16]], axis=0).astype(BF)

    dis_a = Dispatch(send1_a, rx_a, esend_a, emine_a, epart_a, unpack_a)
    dis_b = Dispatch(send1_b, rx_b, esend_b, emine_b, epart_b, unpack_b)
    ret_a = Return(out_a, epin_a, chain_a, etot_a, ein_a, fin_a)
    ret_b = Return(out_b, epin_b, chain_b, etot_b, ein_b, fin_b)
    cut = chunks(6)
    tiles = ff // TILE
    step = min(512, width // PARTS_A)

    routing(1, dd_b, ddt_b, hot_b)
    gates(1, gates_b)
    prepare(hid_b, gates_b, grad_b)
    pack(dd_b, send1_b, rx_b, emine_b, esend_b, columns(nn, 0), columns(gg, 0), width)
    pl.semaphore_wait(barrier, len(greeted))
    dis_b.start_extra()
    dis_b.launch(cut[0])

    routing(0, dd_a, ddt_a, hot_a)
    gates(0, gates_a)
    prepare(hid_a, gates_a, None)
    pack(dd_a, send1_a, rx_a, emine_a, esend_a, columns(nn, 0), columns(nn, half), half)
    ret[272:384, :] = jnp.zeros((112, width), BF)

    dis_b.extra(1)
    dis_a.start_extra()
    dis_b.launch(cut[1])
    for h in range(2, 6):
        dis_b.extra(h)
        dis_a.extra(h - 1)
        dis_b.launch(cut[h])
    dis_a.launch(BLOCKS[:10])
    dis_a.extra(5)
    dis_a.launch(BLOCKS[10:])

    dis_b.collect()
    for copy in weights:
        copy.wait()
    run(backward_units, 0, tiles)
    run(backward_out, 0, half // TILE)
    cut = chunks(4)
    ret_b.swap()
    ret_b.launch(0, cut[0])
    ret_b.extra(1)
    ret_b.launch(0, cut[1])
    dis_a.collect()
    ret_b.extra(2)
    ret_b.launch(0, cut[2])
    run(forward_units, 0, tiles)
    ret_b.extra(3)
    ret_b.launch(0, cut[3])
    for part in range(PARTS_A):
        run(forward_out(part), 0, out_a.shape[3] // TILE)
    ret_b.extra(4)
    ret_a.swap()
    ret_a.launch(0, cut[0])
    ret_a.extra(1)
    ret_a.launch(0, cut[1])
    ret_b.finish_extra()
    ret_a.extra(2)
    ret_a.launch(0, cut[2])
    ret_a.extra(3)
    ret_a.launch(0, cut[3])
    ret_a.extra(4)
    for part in range(1, PARTS_A):
        ret_a.launch(part, BLOCKS)

    ret_b.collect(0)

    @pl.loop(0, width // step)
    def _(i):
        cols = pl.ds(pl.multiple_of(i * step, step), step)
        moved = dot(ddt_b[...], ret[:, cols])
        dnorm[:, cols] = moved[0:tokens] + moved[tokens:]

    @pl.loop(0, tokens // 16)
    def _(i):
        rows = pl.ds(pl.multiple_of(i * 16, 16), 16)
        values = hid_b[rows, :].astype(F32)
        r = inverse_norm(values)
        scaled = dnorm[rows, :] * gain_ref[...]
        inner = jnp.mean(values * scaled, axis=-1, keepdims=True)
        grown = grad_b[rows, :].astype(F32) + r * scaled - values * (r * r * r * inner)
        pipe_b[rows, :] = grown.astype(BF)

    to_prev = describe(pipe_b, prev_ref, pipe_prev)
    if pipes > 1:
        @pl.when(pipe > 0)
        def _():
            to_prev.start()

    ret_a.finish_extra()
    to_next = []
    wide = width // PARTS_A
    for part in range(PARTS_A):
        ret_a.collect(part)

        @pl.loop(0, wide // step)
        def _(i):
            cols = pl.ds(pl.multiple_of(part * wide + i * step, step), step)
            moved = dot(ddt_a[...], ret[:, cols])
            summed = gates_a[0, :, 0:1] * moved[0:tokens] + gates_a[1, :, 0:1] * moved[tokens:]
            pipe_a[:, cols] = (hid_a[:, cols].astype(F32) + summed).astype(BF)

        cols = pl.ds(part * wide, wide)
        copy = describe(pipe_a.at[:, cols], next_ref.at[:, cols], pipe_next)
        to_next.append(copy)
        if pipes > 1:
            @pl.when(pipe < pipes - 1)
            def _():
                copy.start()

    @pl.when(pipe == 0)
    def _():
        next_ref[...] = jnp.zeros(next_ref.shape, BF)

    @pl.when(pipe == pipes - 1)
    def _():
        prev_ref[...] = jnp.zeros(prev_ref.shape, BF)

    for copy in sent:
        copy.wait_send()
    if pipes > 1:
        @pl.when(pipe < pipes - 1)
        def _():
            to_prev.wait_recv()
            for copy in to_next:
                copy.wait_send()

        @pl.when(pipe > 0)
        def _():
            to_prev.wait_send()
            for copy in to_next:
                copy.wait_recv()


def hand_over(first, second, first_out, second_out):
    first_out[...] = first[...]
    second_out[...] = second[...]


def scratch(tokens, width, ff):
    half = width // 2
    vmem = pltpu.VMEM
    part = half // PARTS_A
    shapes = [
        ((width, ff), BF), ((width, ff), BF), ((ff, width), BF),
        ((2 * tokens, width), BF), ((2 * tokens, width), BF),
        ((384, 2 * tokens), BF), ((384, 2 * tokens), BF),
        ((2 * tokens, 384), BF), ((2 * tokens, 384), BF),
        ((32, TILE), F32), ((32, TILE), F32),
        ((2, tokens, tokens), F32), ((2, tokens, tokens), F32),
        ((8, 4, 16, half), BF), ((8, 4, 16, width), BF),
        ((8, 4, 16, half), BF), ((8, 4, 16, width), BF),
        ((16, half), BF), ((16, width), BF),
        ((8, 2, 16, half), BF), ((8, 2, 16, width), BF),
        ((8, 2, 16, half), BF), ((8, 2, 16, width), BF),
        ((512, width), BF), ((512, width), BF), ((512, width), BF),
        ((512, ff), BF), ((512, ff), BF),
        ((PARTS_A, 64, 16, part), BF), ((1, 64, 16, half), BF),
        ((PARTS_A, 16, 16, part), BF), ((1, 16, 16, half), BF),
        ((7, PARTS_A, 2, 16, part), BF), ((7, 1, 2, 16, half), BF),
        ((PARTS_A, 2, 16, part), BF), ((1, 2, 16, half), BF),
        ((PARTS_A, 16, part), BF), ((1, 16, half), BF),
        ((PARTS_A, 8, 4, 16, part), BF), ((1, 8, 4, 16, half), BF),
        ((384, width), BF), ((tokens, width), F32),
        ((tokens, width), BF), ((tokens, width), BF),
    ]
    messages = 256
    return [vmem(shape, kind) for shape, kind in shapes] + [
        pltpu.SemaphoreType.DMA((messages,)),
        pltpu.SemaphoreType.DMA((messages,)),
        pltpu.SemaphoreType.DMA((3,)),
    ]


def per_device(
    hidden_a, expert_ids_a, router_probs_a, hidden_b, expert_ids_b, router_probs_b,
    grad_out_b, norm_gain, w_gate, w_up, w_down,
):
    tokens, width = hidden_a.shape[1:]
    ff = w_gate.shape[3]
    ids = jnp.swapaxes(jnp.concatenate([expert_ids_a, expert_ids_b], axis=0), 1, 2)
    probs = jnp.swapaxes(jnp.concatenate([router_probs_a, router_probs_b], axis=0), 1, 2)
    inside = pl.BlockSpec(memory_space=pltpu.VMEM)
    outside = pl.BlockSpec(memory_space=pl.ANY)
    result = jax.ShapeDtypeStruct((tokens, width), BF)
    rows = 512
    next_hidden, grad_before = pl.pallas_call(
        kernel,
        out_shape=(result, result),
        in_specs=[inside] * 6 + [outside] * 3,
        out_specs=(inside, inside),
        scratch_shapes=scratch(tokens, width, ff),
        compiler_params=pltpu.CompilerParams(
            collective_id=0, has_side_effects=True, vmem_limit_bytes=60 * 1024 * 1024
        ),
        cost_estimate=pl.CostEstimate(
            flops=2 * rows * width * ff * 8, bytes_accessed=6 * width * ff, transcendentals=0
        ),
    )(
        ids, probs, hidden_a[0], hidden_b[0], grad_out_b[0],
        norm_gain, w_gate[0, 0], w_up[0, 0], w_down[0, 0],
    )
    next_hidden, grad_before = pl.pallas_call(
        hand_over,
        out_shape=(result, result),
        in_specs=[inside] * 2,
        out_specs=(inside, inside),
    )(next_hidden, grad_before)
    return next_hidden[None], grad_before[None]


def solution(mesh):
    in_specs = (
        P("pipe", "expert", None),
        P("pipe", "expert", None),
        P("pipe", "expert", None),
        P("pipe", "expert", None),
        P("pipe", "expert", None),
        P("pipe", "expert", None),
        P("pipe", "expert", None),
        P("pipe", None),
        P("pipe", "expert", None, None),
        P("pipe", "expert", None, None),
        P("pipe", "expert", None, None),
    )
    out_specs = (P("pipe", "expert", None), P("pipe", "expert", None))
    return jax.shard_map(
        per_device, mesh=mesh, in_specs=in_specs, out_specs=out_specs, check_vma=False
    )
```

```python
import jax
import jax.numpy as jnp
from jax import lax
from jax.experimental import pallas as pl
from jax.experimental.pallas import tpu as pltpu
from jax.sharding import PartitionSpec as P

NORM_EPS = 1e-06
MESH = pl.DeviceIdType.MESH
BF = jnp.bfloat16
F32 = jnp.float32
RING = 8
ORDER = (4, 3, 5, 2, 6, 1, 7, 0)
PLACE = {k: s for s, k in enumerate(ORDER)}
TILE = 256
PARTS_A = 4
BLOCKS = [(k, q) for k in ORDER for q in (2, 3, 0, 1) if (k, q) != (0, 0)]
SEMAPHORES = 91
EXTRA_HOPS = {"L": 4, "S": 3}


def chunks(count):
    size = -(-len(BLOCKS) // count)
    return [BLOCKS[i:i + size] for i in range(0, len(BLOCKS), size)]


def last_dot(left, right):
    return lax.dot_general(left, right, (((1,), (1,)), ((), ())), preferred_element_type=F32)


def dot(left, right):
    return jnp.dot(left, right, preferred_element_type=F32)


def kernel(
    ids_a_hbm, ids_b_hbm, probs_a_hbm, probs_b_hbm, hid_a_hbm, hid_b_hbm, grad_b_hbm, gain_hbm,
    wg_hbm, wu_hbm, wd_hbm,
    next_ref, prev_ref,
    ids_a, ids_b, probs_a, probs_b, hid_a, hid_b, grad_b, gain_ref, wg, wu, wd, nn, gg, dd_a, dd_b, ddt_a, ddt_b, hot_a, hot_b, gates_a, gates_b,
    send1_a, send1_b, rx_a, rx_b, esend_a, esend_b, emine_a, emine_b, epart_a, epart_b,
    x_a, x_b, s_b, hid1, hid2, out_a, out_b, epin_a, epin_b,
    chain_a, chain_b, etot_a, etot_b, ein_a, ein_b, fin_a, fin_b,
    ret, dnorm, pipe_a, pipe_b, sems,
):
    pipe = lax.axis_index("pipe")
    pipes = lax.axis_size("pipe")
    me = lax.axis_index("expert")
    core = lax.rem(me, 2)
    z = lax.rem(lax.div(me, 2), RING)
    x = lax.div(me, 2 * RING)
    sg = 1 - 2 * core
    width = hid_a.shape[1]
    half = width // 2
    ff = wg.shape[1]
    tokens = hid_a.shape[0]

    def device(xx, zz, cc):
        return {"expert": (xx * RING + zz) * 2 + cc}

    partner = [
        device(x if q < 2 else 1 - x, z, core if q % 2 == 0 else 1 - core) for q in range(4)
    ]

    def target(k, q):
        cc = core if q % 2 == 0 else 1 - core
        return device(x if q < 2 else 1 - x, lax.rem(z + (1 - 2 * cc) * k + RING, RING), cc)

    def source(k, q):
        cc = core if q % 2 == 0 else 1 - core
        return device(x if q < 2 else 1 - x, lax.rem(z - sg * k + RING, RING), cc)

    long_way = device(x, lax.rem(z + sg + RING, RING), core)
    short_way = device(x, lax.rem(z - sg + RING, RING), core)
    pipe_next = {"pipe": lax.rem(pipe + 1, pipes)}
    pipe_prev = {"pipe": lax.rem(pipe + pipes - 1, pipes)}

    used = [0]
    unwaited = []

    def semaphores(count):
        first = used[0]
        used[0] += count
        return [sems.at[first + i] for i in range(count)]

    def wait_for(ref, sem):
        pltpu.make_async_copy(ref, ref, sem).wait()

    def send(src, dst, where, send_sem, recv_sem):
        copy = pltpu.make_async_remote_copy(
            src_ref=src, dst_ref=dst, send_sem=send_sem, recv_sem=recv_sem,
            device_id=where, device_id_type=MESH,
        )
        copy.start()

    barrier = pltpu.get_barrier_semaphore()
    greeted = [target(k, q) for k, q in BLOCKS]
    if pipes > 1:
        greeted += [pipe_next, pipe_prev]
    for other in greeted:
        pl.semaphore_signal(barrier, inc=1, device_id=other, device_id_type=MESH)

    def fetch(src, dst):
        copy = pltpu.make_async_copy(src, dst, semaphores(1)[0])
        copy.start()
        return copy

    got_b = [
        fetch(*pair) for pair in (
            (ids_b_hbm, ids_b), (probs_b_hbm, probs_b), (gain_hbm, gain_ref),
            (hid_b_hbm, hid_b), (grad_b_hbm, grad_b),
        )
    ]
    got_a = [
        fetch(*pair) for pair in ((ids_a_hbm, ids_a), (probs_a_hbm, probs_a), (hid_a_hbm, hid_a))
    ]
    weights = [fetch(*pair) for pair in ((wg_hbm, wg), (wu_hbm, wu), (wd_hbm, wd))]

    def routing(ids_ref, dd, ddt, hot):
        ids = ids_ref[...]
        j = lax.broadcasted_iota(jnp.int32, (32, tokens), 0)
        q = j & 3
        s = j >> 2
        k = jnp.where((s & 1) == 1, 3 - (s >> 1), 4 + (s >> 1))
        cq = (core + (q & 1)) & 1
        xq = (x + (q >> 1)) & 1
        zq = (z + (1 - 2 * cq) * k + RING) & (RING - 1)
        expert = (xq * RING + zq) * 2 + cq
        match = (ids[0:1, :] == expert) | (ids[1:2, :] == expert)
        matched = jnp.where(match, 1.0, 0.0)
        t0 = lax.broadcasted_iota(jnp.int32, (tokens, tokens), 0)
        t1 = lax.broadcasted_iota(jnp.int32, (tokens, tokens), 1)
        rank = dot(matched.astype(BF), jnp.where(t0 < t1, 1.0, 0.0).astype(BF))
        ranked = jnp.where(match, rank, 200.0)
        own = q < 2
        rank_own = jnp.sum(jnp.where(own, matched * rank, 0.0), axis=0, keepdims=True)
        rank_other = jnp.sum(jnp.where(own, 0.0, matched * rank), axis=0, keepdims=True)
        hot[...] = dot(matched.astype(BF), jnp.ones((tokens, TILE), BF))
        r = lax.broadcasted_iota(jnp.int32, (256, 32), 0)
        cols = lax.broadcasted_iota(jnp.int32, (256, 32), 1)
        spread = jnp.where((r >> 3) == cols, 1.0, 0.0).astype(BF)
        rows = dot(spread, ranked.astype(BF))
        r = lax.broadcasted_iota(jnp.int32, (256, tokens), 0)
        hit = rows == (r & 7).astype(F32)
        mine = ((r >> 3) & 3) < 2
        dd[0:256, 0:tokens] = jnp.where(hit & mine, 1.0, 0.0).astype(BF)
        dd[0:256, tokens:] = jnp.where(hit & jnp.logical_not(mine), 1.0, 0.0).astype(BF)
        r = lax.broadcasted_iota(jnp.int32, (128, tokens), 0)
        rf = r.astype(F32)
        dd[256:384, 0:tokens] = jnp.where((rank_own == rf + 8.0) & (r < 8), 1.0, 0.0).astype(BF)
        dd[256:384, tokens:] = jnp.where(
            (rank_other == rf) & (r >= 8) & (r < 16), 1.0, 0.0
        ).astype(BF)
        t0 = lax.broadcasted_iota(jnp.int32, (2 * tokens, 2 * tokens), 0)
        t1 = lax.broadcasted_iota(jnp.int32, (2 * tokens, 2 * tokens), 1)
        eye = jnp.where(t0 == t1, 1.0, 0.0).astype(BF)
        ddt[...] = last_dot(eye, dd[...]).astype(BF)

    xf = x.astype(F32)

    def gates(probs_ref, gate):
        probs = probs_ref[...]
        weight = probs / jnp.sum(probs, axis=0, keepdims=True)
        first, second = weight[0:1, :], weight[1:2, :]
        for i, row in enumerate(
            (first * (1.0 - xf) + second * xf, second * (1.0 - xf) + first * xf)
        ):
            gate[i] = jnp.broadcast_to(row, (tokens, tokens)).T

    def inverse_norm(values):
        return lax.rsqrt(jnp.mean(values * values, axis=-1, keepdims=True) + NORM_EPS)

    def prepare(hidden, gate, gradient):
        @pl.loop(0, tokens // 16)
        def _(i):
            rows = pl.ds(pl.multiple_of(i * 16, 16), 16)
            later = pl.ds(pl.multiple_of(tokens + i * 16, 16), 16)
            values = hidden[rows, :].astype(F32)
            normed = (values * inverse_norm(values) * gain_ref[...]).astype(BF)
            nn[rows, :] = normed
            nn[later, :] = normed
            if gradient is not None:
                up = gradient[rows, :].astype(F32)
                gg[rows, :] = (gate[0, rows, 0:1] * up).astype(BF)
                gg[later, :] = (gate[1, rows, 0:1] * up).astype(BF)

    def pack(dd, send1, rx, emine, esend, first, second, wide):
        step = min(512, wide)

        @pl.loop(0, wide // step)
        def _(i):
            cols = pl.ds(pl.multiple_of(i * step, step), step)
            top = dot(dd[0:272, :], first(i * step, step))
            low = dot(dd[0:272, :], second(i * step, step))
            both = jnp.concatenate(
                [top.reshape(34, 8, step), low.reshape(34, 8, step)], axis=1
            ).astype(BF)
            send1[:, :, :, cols] = both[0:32].reshape(8, 4, 16, step)
            rx[0, 0, :, cols] = both[4 * PLACE[0]]
            emine[0, 0, :, cols] = both[32]
            esend[:, cols] = both[33]

    def columns(ref, base):
        def take(start, size):
            return ref[:, pl.ds(pl.multiple_of(base + start, size), size)]

        return take

    class Dispatch:
        def __init__(self, send1, rx, esend, emine, epart, unpack):
            self.send1, self.rx, self.esend, self.emine = send1, rx, esend, emine
            self.epart, self.unpack = epart, unpack
            self.main_sem = semaphores(RING)
            self.hop_sem = {"L": semaphores(4), "S": semaphores(3)}
            self.first_sem, self.part_sem = semaphores(2)
            self.sent_first, self.sent_hop, self.sent_part = semaphores(3)
            self.sent_far, self.sent_near = semaphores(2)
            unwaited.extend([
                (rx.at[pl.ds(1, 7)], self.sent_far), (rx.at[0, pl.ds(1, 3)], self.sent_near),
                (esend, self.sent_first), (emine.at[pl.ds(0, 7)], self.sent_hop),
                (emine, self.sent_part),
            ])

        def launch(self, blocks):
            for k, q in blocks:
                send(
                    self.send1.at[PLACE[k], q], self.rx.at[k, q], target(k, q),
                    self.sent_far if k else self.sent_near, self.main_sem[k],
                )

        def start_extra(self):
            send(self.esend, self.emine.at[0, 1], partner[2], self.sent_first, self.first_sem)

        def swap_extra(self, k):
            send(self.emine.at[k], self.epart.at[k], partner[1], self.sent_part, self.part_sem)

        def extra(self, h):
            if h == 1:
                wait_for(self.emine.at[0, 1], self.first_sem)
            for way, last in EXTRA_HOPS.items():
                if 1 < h <= last + 1:
                    wait_for(self.emine.at[0], self.hop_sem[way][h - 2])
                if h <= last:
                    a, b = (h - 1, h) if way == "L" else ((9 - h) % RING, RING - h)
                    send(
                        self.emine.at[a], self.emine.at[b],
                        long_way if way == "L" else short_way,
                        self.sent_hop, self.hop_sem[way][h - 1],
                    )
            if h <= 5:
                for k in {h - 1, (9 - h) % RING} if h <= 4 else {4}:
                    self.swap_extra(k)

        def collect(self):
            for k in ORDER:
                arrived = self.rx.at[k] if k else self.rx.at[0, pl.ds(1, 3)]
                wait_for(arrived, self.main_sem[k])
                self.unpack(self.rx.at[k], k * 32)
            wait_for(self.epart, self.part_sem)
            for k in range(RING):
                self.unpack(self.emine.at[k], 256 + k * 16)
                self.unpack(self.epart.at[k], 384 + k * 16)

    def unpack_b(src, row):
        count = src.shape[0]
        values = src[...].astype(F32).reshape(count, 2, 8, width)
        rows = pl.ds(row, count * 8)
        x_b[rows, :] = values[:, 0].reshape(count * 8, width).astype(BF)
        s_b[rows, :] = values[:, 1].reshape(count * 8, width).astype(BF)

    def unpack_a(src, row):
        count = src.shape[0]
        values = src[...].astype(F32).reshape(count, 2, 8, half)
        rows = pl.ds(row, count * 8)
        x_a[rows, 0:half] = values[:, 0].reshape(count * 8, half).astype(BF)
        x_a[rows, half:] = values[:, 1].reshape(count * 8, half).astype(BF)

    def tile_at(i):
        return pl.ds(pl.multiple_of(i * TILE, TILE), TILE)

    def forward_units(i):
        cols = tile_at(i)
        gate_pre = dot(x_a[...], wg[:, cols])
        up_pre = dot(x_a[...], wu[:, cols])
        hid1[:, cols] = (gate_pre * jax.nn.sigmoid(gate_pre) * up_pre).astype(BF)

    def backward_units(i):
        cols = tile_at(i)
        gate_pre = dot(x_b[...], wg[:, cols])
        up_pre = dot(x_b[...], wu[:, cols])
        d_hidden = last_dot(s_b[...], wd[cols, :])
        sigma = jax.nn.sigmoid(gate_pre)
        hid1[:, cols] = (d_hidden * up_pre * sigma * (1.0 + gate_pre * (1.0 - sigma))).astype(BF)
        hid2[:, cols] = (d_hidden * gate_pre * sigma).astype(BF)

    def store_out(out, part, hot, i, low, high):
        valid = jnp.broadcast_to(hot[28:29, :], (256, TILE)) > 8.5
        both = []
        for half_rows in (low, high):
            extra = jnp.where(valid, half_rows[256:512], 0.0)
            both.append(
                jnp.concatenate([half_rows[0:256], extra], axis=0).reshape(64, 8, TILE)
            )
        out[part, :, :, tile_at(i)] = jnp.concatenate(both, axis=1).astype(BF)

    def shifted(base, i):
        return pl.ds(pl.multiple_of(base + i * TILE, TILE), TILE)

    def forward_out(part):
        wide = out_a.shape[3]

        def step(i):
            low = dot(hid1[...], wd[:, shifted(2 * part * wide, i)])
            high = dot(hid1[...], wd[:, shifted((2 * part + 1) * wide, i)])
            store_out(out_a, part, hot_a, i, low, high)

        return step

    def backward_out(i):
        now, later = shifted(0, i), shifted(half, i)
        low = last_dot(hid1[...], wg[now, :]) + last_dot(hid2[...], wu[now, :])
        high = last_dot(hid1[...], wg[later, :]) + last_dot(hid2[...], wu[later, :])
        store_out(out_b, 0, hot_b, i, low, high)

    def run(step, first, last):
        @pl.loop(first, last)
        def _(i):
            step(i)

    class Return:
        def __init__(self, out, epin, chain, etot, ein, fin):
            self.out, self.epin, self.chain = out, epin, chain
            self.etot, self.ein, self.fin = etot, ein, fin
            self.main_sem = semaphores(out.shape[0])
            self.hop_sem = {"L": semaphores(4), "S": semaphores(3)}
            self.swap_sem, self.last_sem = semaphores(2)
            self.sent_main, self.sent_hop, self.sent_swap, self.sent_last = semaphores(4)
            unwaited.extend([
                (fin, self.sent_main), (chain, self.sent_hop), (epin, self.sent_swap),
                (ein, self.sent_last),
            ])

        def launch(self, part, blocks):
            for k, q in blocks:
                send(
                    self.out.at[part, 4 * k + q], self.fin.at[part, 4 * k + q - 1], source(k, q),
                    self.sent_main, self.main_sem[part],
                )

        def swap(self):
            send(
                self.out.at[:, pl.ds(48, 16)], self.epin, partner[1],
                self.sent_swap, self.swap_sem,
            )

        def hop(self, way, h, src, dst):
            send(
                src, dst, short_way if way == "L" else long_way,
                self.sent_hop, self.hop_sem[way][h - 1],
            )

        def extra(self, h):
            if h == 1:
                wait_for(self.epin, self.swap_sem)
                mine = self.out[:, 32:48].astype(F32)
                self.epin[...] = (mine + self.epin[...].astype(F32)).astype(BF)
                self.hop("L", 1, self.epin.at[:, pl.ds(8, 2)], self.chain.at[0])
                self.hop("S", 1, self.epin.at[:, pl.ds(10, 2)], self.chain.at[4])
                return
            for way, last in EXTRA_HOPS.items():
                if h > last:
                    continue
                k, at = (5 - h, h - 2) if way == "L" else (4 + h, 2 + h)
                wait_for(self.chain.at[at], self.hop_sem[way][h - 2])
                mine = self.epin[:, 2 * k:2 * k + 2].astype(F32)
                self.chain[at] = (self.chain[at].astype(F32) + mine).astype(BF)
                self.hop(way, h, self.chain.at[at], self.chain.at[at + 1])

        def finish_extra(self):
            wait_for(self.chain.at[3], self.hop_sem["L"][3])
            wait_for(self.chain.at[6], self.hop_sem["S"][2])
            total = self.epin[:, 0:2].astype(F32) + self.chain[3].astype(F32)
            self.etot[...] = (total + self.chain[6].astype(F32)).astype(BF)
            send(self.etot.at[:, 1], self.ein, partner[2], self.sent_last, self.last_sem)

        def collect(self, part):
            wide = self.out.shape[3]
            low = pl.ds(2 * part * wide, wide)
            high = pl.ds((2 * part + 1) * wide, wide)
            wait_for(self.fin.at[part], self.main_sem[part])
            for k in range(RING):
                if k == 0:
                    own = self.out[part, 0:1].astype(F32)
                    block = jnp.concatenate([own, self.fin[part, 0:3].astype(F32)], axis=0)
                else:
                    block = self.fin[part, 4 * k - 1:4 * k + 3].astype(F32)
                block = block.reshape(4, 2, 8, wide)
                rows = pl.ds(PLACE[k] * 32, 32)
                ret[rows, low] = block[:, 0].reshape(32, wide).astype(BF)
                ret[rows, high] = block[:, 1].reshape(32, wide).astype(BF)
            if part == 0:
                wait_for(self.ein, self.last_sem)
            own, other = self.etot[part, 0].astype(F32), self.ein[part].astype(F32)
            ret[256:272, low] = jnp.concatenate([own[0:8], other[0:8]], axis=0).astype(BF)
            ret[256:272, high] = jnp.concatenate([own[8:16], other[8:16]], axis=0).astype(BF)

    dis_a = Dispatch(send1_a, rx_a, esend_a, emine_a, epart_a, unpack_a)
    dis_b = Dispatch(send1_b, rx_b, esend_b, emine_b, epart_b, unpack_b)
    ret_a = Return(out_a, epin_a, chain_a, etot_a, ein_a, fin_a)
    ret_b = Return(out_b, epin_b, chain_b, etot_b, ein_b, fin_b)
    cut = chunks(6)
    tiles = ff // TILE
    step = min(512, width // PARTS_A)

    for copy in got_b:
        copy.wait()
    routing(ids_b, dd_b, ddt_b, hot_b)
    gates(probs_b, gates_b)
    prepare(hid_b, gates_b, grad_b)
    pack(dd_b, send1_b, rx_b, emine_b, esend_b, columns(nn, 0), columns(gg, 0), width)
    pl.semaphore_wait(barrier, len(greeted))
    dis_b.start_extra()
    dis_b.launch(cut[0])

    for copy in got_a:
        copy.wait()
    routing(ids_a, dd_a, ddt_a, hot_a)
    gates(probs_a, gates_a)
    prepare(hid_a, gates_a, None)
    pack(dd_a, send1_a, rx_a, emine_a, esend_a, columns(nn, 0), columns(nn, half), half)
    ret[272:384, :] = jnp.zeros((112, width), BF)
    prev_sent, prev_got, next_sent, next_got, zero_sem = semaphores(5)

    def blank(ref):
        nn[0:tokens, :] = jnp.zeros((tokens, width), BF)
        pltpu.make_async_copy(nn.at[pl.ds(0, tokens)], ref, zero_sem).start()
        pltpu.make_async_copy(nn.at[pl.ds(0, tokens)], ref, zero_sem).wait()

    @pl.when(pipe == 0)
    def _():
        blank(next_ref)

    @pl.when(pipe == pipes - 1)
    def _():
        blank(prev_ref)

    dis_b.extra(1)
    dis_a.start_extra()
    dis_b.launch(cut[1])
    for h in range(2, 6):
        dis_b.extra(h)
        dis_a.extra(h - 1)
        dis_b.launch(cut[h])
    dis_a.launch(BLOCKS[:10])
    dis_a.extra(5)
    dis_a.launch(BLOCKS[10:])

    dis_b.collect()
    for copy in weights:
        copy.wait()
    run(backward_units, 0, tiles)
    run(backward_out, 0, half // TILE)
    ret_b.swap()
    ret_b.launch(0, BLOCKS[:8])
    dis_a.collect()
    ret_b.launch(0, BLOCKS[8:14])
    run(forward_units, 0, tiles)
    for part in range(PARTS_A):
        run(forward_out(part), 0, out_a.shape[3] // TILE)
    ret_a.swap()
    for h, (start, end) in enumerate(((14, 20), (20, 26), (26, 31), (31, 31))):
        ret_b.extra(h + 1)
        ret_a.extra(h + 1)
        ret_b.launch(0, BLOCKS[start:end])
    ret_a.launch(0, BLOCKS)
    ret_b.finish_extra()
    ret_a.finish_extra()
    for part in range(1, PARTS_A):
        ret_a.launch(part, BLOCKS)

    ret_b.collect(0)

    @pl.loop(0, width // step)
    def _(i):
        cols = pl.ds(pl.multiple_of(i * step, step), step)
        moved = dot(ddt_b[...], ret[:, cols])
        dnorm[:, cols] = moved[0:tokens] + moved[tokens:]

    @pl.loop(0, tokens // 16)
    def _(i):
        rows = pl.ds(pl.multiple_of(i * 16, 16), 16)
        values = hid_b[rows, :].astype(F32)
        r = inverse_norm(values)
        scaled = dnorm[rows, :] * gain_ref[...]
        inner = jnp.mean(values * scaled, axis=-1, keepdims=True)
        grown = grad_b[rows, :].astype(F32) + r * scaled - values * (r * r * r * inner)
        pipe_b[rows, :] = grown.astype(BF)

    if pipes > 1:
        @pl.when(pipe > 0)
        def _():
            send(pipe_b, prev_ref, pipe_prev, prev_sent, prev_got)

    wide = width // PARTS_A
    for part in range(PARTS_A):
        ret_a.collect(part)

        @pl.loop(0, wide // step)
        def _(i):
            cols = pl.ds(pl.multiple_of(part * wide + i * step, step), step)
            moved = dot(ddt_a[...], ret[:, cols])
            summed = gates_a[0, :, 0:1] * moved[0:tokens] + gates_a[1, :, 0:1] * moved[tokens:]
            pipe_a[:, cols] = (hid_a[:, cols].astype(F32) + summed).astype(BF)

        cols = pl.ds(part * wide, wide)
        if pipes > 1:
            @pl.when(pipe < pipes - 1)
            def _():
                send(pipe_a.at[:, cols], next_ref.at[:, cols], pipe_next, next_sent, next_got)

    for ref, sem in unwaited:
        wait_for(ref, sem)
    if pipes > 1:
        @pl.when(pipe < pipes - 1)
        def _():
            wait_for(prev_ref, prev_got)
            wait_for(pipe_a, next_sent)

        @pl.when(pipe > 0)
        def _():
            wait_for(pipe_b, prev_sent)
            wait_for(next_ref, next_got)


def hand_over(first, second, first_out, second_out):
    first_out[...] = first[...]
    second_out[...] = second[...]


def scratch(tokens, width, ff):
    half = width // 2
    vmem = pltpu.VMEM
    part = half // PARTS_A
    shapes = [
        ((width, ff), BF), ((width, ff), BF), ((ff, width), BF),
        ((2 * tokens, width), BF), ((2 * tokens, width), BF),
        ((384, 2 * tokens), BF), ((384, 2 * tokens), BF),
        ((2 * tokens, 384), BF), ((2 * tokens, 384), BF),
        ((32, TILE), F32), ((32, TILE), F32),
        ((2, tokens, tokens), F32), ((2, tokens, tokens), F32),
        ((8, 4, 16, half), BF), ((8, 4, 16, width), BF),
        ((8, 4, 16, half), BF), ((8, 4, 16, width), BF),
        ((16, half), BF), ((16, width), BF),
        ((8, 2, 16, half), BF), ((8, 2, 16, width), BF),
        ((8, 2, 16, half), BF), ((8, 2, 16, width), BF),
        ((512, width), BF), ((512, width), BF), ((512, width), BF),
        ((512, ff), BF), ((512, ff), BF),
        ((PARTS_A, 64, 16, part), BF), ((1, 64, 16, half), BF),
        ((PARTS_A, 16, 16, part), BF), ((1, 16, 16, half), BF),
        ((7, PARTS_A, 2, 16, part), BF), ((7, 1, 2, 16, half), BF),
        ((PARTS_A, 2, 16, part), BF), ((1, 2, 16, half), BF),
        ((PARTS_A, 16, part), BF), ((1, 16, half), BF),
        ((PARTS_A, 31, 16, part), BF), ((1, 31, 16, half), BF),
        ((384, width), BF), ((tokens, width), F32),
        ((tokens, width), BF), ((tokens, width), BF),
    ]
    arguments = [
        ((8, tokens), jnp.int32), ((8, tokens), jnp.int32), ((8, tokens), F32), ((8, tokens), F32),
        ((tokens, width), BF), ((tokens, width), BF), ((tokens, width), BF), ((1, width), F32),
    ]
    return [vmem(shape, kind) for shape, kind in arguments + shapes] + [
        pltpu.SemaphoreType.DMA((SEMAPHORES,))
    ]


def per_device(
    hidden_a, expert_ids_a, router_probs_a, hidden_b, expert_ids_b, router_probs_b,
    grad_out_b, norm_gain, w_gate, w_up, w_down,
):
    tokens, width = hidden_a.shape[1:]
    ff = w_gate.shape[3]
    small = [
        jnp.swapaxes(value[0], 0, 1)
        for value in (expert_ids_a, expert_ids_b, router_probs_a, router_probs_b)
    ]
    inside = pl.BlockSpec(memory_space=pltpu.VMEM)
    outside = pl.BlockSpec(memory_space=pl.ANY)
    result = jax.ShapeDtypeStruct((tokens, width), BF)
    rows = 512
    next_hidden, grad_before = pl.pallas_call(
        kernel,
        out_shape=(result, result),
        in_specs=[outside] * 11,
        out_specs=(outside, outside),
        scratch_shapes=scratch(tokens, width, ff),
        compiler_params=pltpu.CompilerParams(
            collective_id=0, has_side_effects=True, vmem_limit_bytes=60 * 1024 * 1024
        ),
        cost_estimate=pl.CostEstimate(
            flops=2 * rows * width * ff * 8, bytes_accessed=6 * width * ff, transcendentals=0
        ),
    )(
        *small, hidden_a[0], hidden_b[0], grad_out_b[0],
        norm_gain, w_gate[0, 0], w_up[0, 0], w_down[0, 0],
    )
    next_hidden, grad_before = pl.pallas_call(
        hand_over,
        out_shape=(result, result),
        in_specs=[inside] * 2,
        out_specs=(inside, inside),
    )(next_hidden, grad_before)
    return next_hidden[None], grad_before[None]


def solution(mesh):
    in_specs = (
        P("pipe", "expert", None),
        P("pipe", "expert", None),
        P("pipe", "expert", None),
        P("pipe", "expert", None),
        P("pipe", "expert", None),
        P("pipe", "expert", None),
        P("pipe", "expert", None),
        P("pipe", None),
        P("pipe", "expert", None, None),
        P("pipe", "expert", None, None),
        P("pipe", "expert", None, None),
    )
    out_specs = (P("pipe", "expert", None), P("pipe", "expert", None))
    return jax.shard_map(
        per_device, mesh=mesh, in_specs=in_specs, out_specs=out_specs, check_vma=False
    )
```

```python
import jax
import jax.numpy as jnp
from jax import lax
from jax.experimental import pallas as pl
from jax.experimental.pallas import tpu as pltpu
from jax.sharding import PartitionSpec as P

NORM_EPS = 1e-06
MESH = pl.DeviceIdType.MESH
BF = jnp.bfloat16
F32 = jnp.float32
RING = 8
ORDER = (4, 3, 5, 2, 6, 1, 7, 0)
PLACE = {k: s for s, k in enumerate(ORDER)}
TILE = 256
PARTS_A = 8
BLOCKS = [(k, q) for k in ORDER for q in (2, 3, 0, 1) if (k, q) != (0, 0)]
SEMAPHORES = 96
EXTRA_HOPS = {"L": 4, "S": 3}


def chunks(count):
    size = -(-len(BLOCKS) // count)
    return [BLOCKS[i:i + size] for i in range(0, len(BLOCKS), size)]


def last_dot(left, right):
    return lax.dot_general(left, right, (((1,), (1,)), ((), ())), preferred_element_type=F32)


def dot(left, right):
    return jnp.dot(left, right, preferred_element_type=F32)


def kernel(
    ids_a_hbm, ids_b_hbm, probs_a_hbm, probs_b_hbm, hid_a_hbm, hid_b_hbm, grad_b_hbm, gain_hbm,
    wg_hbm, wu_hbm, wd_hbm,
    next_ref, prev_ref,
    ids_a, ids_b, probs_a, probs_b, hid_a, hid_b, grad_b, gain_ref, wg, wu, wd, nn, gg, dd_a, dd_b, ddt_a, ddt_b, hot_a, hot_b, gates_a, gates_b,
    send1_a, send1_b, rx_a, rx_b, esend_a, esend_b, emine_a, emine_b, epart_a, epart_b,
    x_a, x_b, s_b, hid1, hid2, out_a, out_b, oute_a, oute_b, epin_a, epin_b,
    chain_a, chain_b, etot_a, etot_b, ein_a, ein_b, fin_a, fin_b,
    ret, dnorm, pipe_a, pipe_b, sems,
):
    pipe = lax.axis_index("pipe")
    pipes = lax.axis_size("pipe")
    me = lax.axis_index("expert")
    core = lax.rem(me, 2)
    z = lax.rem(lax.div(me, 2), RING)
    x = lax.div(me, 2 * RING)
    sg = 1 - 2 * core
    width = hid_a.shape[1]
    half = width // 2
    ff = wg.shape[1]
    tokens = hid_a.shape[0]

    def device(xx, zz, cc):
        return {"expert": (xx * RING + zz) * 2 + cc}

    partner = [
        device(x if q < 2 else 1 - x, z, core if q % 2 == 0 else 1 - core) for q in range(4)
    ]

    def target(k, q):
        cc = core if q % 2 == 0 else 1 - core
        return device(x if q < 2 else 1 - x, lax.rem(z + (1 - 2 * cc) * k + RING, RING), cc)

    def source(k, q):
        cc = core if q % 2 == 0 else 1 - core
        return device(x if q < 2 else 1 - x, lax.rem(z - sg * k + RING, RING), cc)

    long_way = device(x, lax.rem(z + sg + RING, RING), core)
    short_way = device(x, lax.rem(z - sg + RING, RING), core)
    pipe_next = {"pipe": lax.rem(pipe + 1, pipes)}
    pipe_prev = {"pipe": lax.rem(pipe + pipes - 1, pipes)}

    used = [0]
    unwaited = []

    def semaphores(count):
        first = used[0]
        used[0] += count
        return [sems.at[first + i] for i in range(count)]

    def wait_for(ref, sem):
        pltpu.make_async_copy(ref, ref, sem).wait()

    def send(src, dst, where, send_sem, recv_sem):
        copy = pltpu.make_async_remote_copy(
            src_ref=src, dst_ref=dst, send_sem=send_sem, recv_sem=recv_sem,
            device_id=where, device_id_type=MESH,
        )
        copy.start()

    barrier = pltpu.get_barrier_semaphore()
    greeted = [target(k, q) for k, q in BLOCKS]
    if pipes > 1:
        greeted += [pipe_next, pipe_prev]
    for other in greeted:
        pl.semaphore_signal(barrier, inc=1, device_id=other, device_id_type=MESH)

    def fetch(src, dst):
        copy = pltpu.make_async_copy(src, dst, semaphores(1)[0])
        copy.start()
        return copy

    got_b = [
        fetch(*pair) for pair in (
            (ids_b_hbm, ids_b), (probs_b_hbm, probs_b), (gain_hbm, gain_ref),
            (hid_b_hbm, hid_b), (grad_b_hbm, grad_b),
        )
    ]
    got_a = [
        fetch(*pair) for pair in ((ids_a_hbm, ids_a), (probs_a_hbm, probs_a), (hid_a_hbm, hid_a))
    ]
    weights = [fetch(*pair) for pair in ((wg_hbm, wg), (wu_hbm, wu), (wd_hbm, wd))]

    def routing(ids_ref, dd, ddt, hot):
        ids = ids_ref[...]
        j = lax.broadcasted_iota(jnp.int32, (32, tokens), 0)
        q = j & 3
        s = j >> 2
        k = jnp.where((s & 1) == 1, 3 - (s >> 1), 4 + (s >> 1))
        cq = (core + (q & 1)) & 1
        xq = (x + (q >> 1)) & 1
        zq = (z + (1 - 2 * cq) * k + RING) & (RING - 1)
        expert = (xq * RING + zq) * 2 + cq
        match = (ids[0:1, :] == expert) | (ids[1:2, :] == expert)
        matched = jnp.where(match, 1.0, 0.0)
        t0 = lax.broadcasted_iota(jnp.int32, (tokens, tokens), 0)
        t1 = lax.broadcasted_iota(jnp.int32, (tokens, tokens), 1)
        rank = dot(matched.astype(BF), jnp.where(t0 < t1, 1.0, 0.0).astype(BF))
        ranked = jnp.where(match, rank, 200.0)
        own = q < 2
        rank_own = jnp.sum(jnp.where(own, matched * rank, 0.0), axis=0, keepdims=True)
        rank_other = jnp.sum(jnp.where(own, 0.0, matched * rank), axis=0, keepdims=True)
        hot[...] = dot(matched.astype(BF), jnp.ones((tokens, TILE), BF))
        r = lax.broadcasted_iota(jnp.int32, (256, 32), 0)
        cols = lax.broadcasted_iota(jnp.int32, (256, 32), 1)
        spread = jnp.where((r >> 3) == cols, 1.0, 0.0).astype(BF)
        rows = dot(spread, ranked.astype(BF))
        r = lax.broadcasted_iota(jnp.int32, (256, tokens), 0)
        hit = rows == (r & 7).astype(F32)
        mine = ((r >> 3) & 3) < 2
        dd[0:256, 0:tokens] = jnp.where(hit & mine, 1.0, 0.0).astype(BF)
        dd[0:256, tokens:] = jnp.where(hit & jnp.logical_not(mine), 1.0, 0.0).astype(BF)
        r = lax.broadcasted_iota(jnp.int32, (128, tokens), 0)
        rf = r.astype(F32)
        dd[256:384, 0:tokens] = jnp.where((rank_own == rf + 8.0) & (r < 8), 1.0, 0.0).astype(BF)
        dd[256:384, tokens:] = jnp.where(
            (rank_other == rf) & (r >= 8) & (r < 16), 1.0, 0.0
        ).astype(BF)
        t0 = lax.broadcasted_iota(jnp.int32, (2 * tokens, 2 * tokens), 0)
        t1 = lax.broadcasted_iota(jnp.int32, (2 * tokens, 2 * tokens), 1)
        eye = jnp.where(t0 == t1, 1.0, 0.0).astype(BF)
        ddt[...] = last_dot(eye, dd[...]).astype(BF)

    xf = x.astype(F32)

    def gates(probs_ref, gate):
        probs = probs_ref[...]
        weight = probs / jnp.sum(probs, axis=0, keepdims=True)
        first, second = weight[0:1, :], weight[1:2, :]
        for i, row in enumerate(
            (first * (1.0 - xf) + second * xf, second * (1.0 - xf) + first * xf)
        ):
            gate[i] = jnp.broadcast_to(row, (tokens, tokens)).T

    def inverse_norm(values):
        return lax.rsqrt(jnp.mean(values * values, axis=-1, keepdims=True) + NORM_EPS)

    def prepare(hidden, gate, gradient):
        @pl.loop(0, tokens // 16)
        def _(i):
            rows = pl.ds(pl.multiple_of(i * 16, 16), 16)
            later = pl.ds(pl.multiple_of(tokens + i * 16, 16), 16)
            values = hidden[rows, :].astype(F32)
            normed = (values * inverse_norm(values) * gain_ref[...]).astype(BF)
            nn[rows, :] = normed
            nn[later, :] = normed
            if gradient is not None:
                up = gradient[rows, :].astype(F32)
                gg[rows, :] = (gate[0, rows, 0:1] * up).astype(BF)
                gg[later, :] = (gate[1, rows, 0:1] * up).astype(BF)

    def pack(dd, send1, rx, emine, esend, first, second, wide):
        step = min(512, wide)

        @pl.loop(0, wide // step)
        def _(i):
            cols = pl.ds(pl.multiple_of(i * step, step), step)
            top = dot(dd[0:272, :], first(i * step, step))
            low = dot(dd[0:272, :], second(i * step, step))
            both = jnp.concatenate(
                [top.reshape(34, 8, step), low.reshape(34, 8, step)], axis=1
            ).astype(BF)
            send1[:, :, :, cols] = both[0:32].reshape(8, 4, 16, step)
            rx[0, 0, :, cols] = both[4 * PLACE[0]]
            emine[0, 0, :, cols] = both[32]
            esend[:, cols] = both[33]

    def columns(ref, base):
        def take(start, size):
            return ref[:, pl.ds(pl.multiple_of(base + start, size), size)]

        return take

    class Dispatch:
        def __init__(self, send1, rx, esend, emine, epart, unpack):
            self.send1, self.rx, self.esend, self.emine = send1, rx, esend, emine
            self.epart, self.unpack = epart, unpack
            self.main_sem = semaphores(RING)
            self.hop_sem = {"L": semaphores(4), "S": semaphores(3)}
            self.first_sem, self.part_sem = semaphores(2)
            self.sent_first, self.sent_hop, self.sent_part = semaphores(3)
            self.sent_far, self.sent_near = semaphores(2)
            unwaited.extend([
                (rx.at[pl.ds(1, 7)], self.sent_far), (rx.at[0, pl.ds(1, 3)], self.sent_near),
                (esend, self.sent_first), (emine.at[pl.ds(0, 7)], self.sent_hop),
                (emine, self.sent_part),
            ])

        def launch(self, blocks):
            for k, q in blocks:
                send(
                    self.send1.at[PLACE[k], q], self.rx.at[k, q], target(k, q),
                    self.sent_far if k else self.sent_near, self.main_sem[k],
                )

        def start_extra(self):
            send(self.esend, self.emine.at[0, 1], partner[2], self.sent_first, self.first_sem)

        def swap_extra(self, k):
            send(self.emine.at[k], self.epart.at[k], partner[1], self.sent_part, self.part_sem)

        def extra(self, h):
            if h == 1:
                wait_for(self.emine.at[0, 1], self.first_sem)
            for way, last in EXTRA_HOPS.items():
                if 1 < h <= last + 1:
                    wait_for(self.emine.at[0], self.hop_sem[way][h - 2])
                if h <= last:
                    a, b = (h - 1, h) if way == "L" else ((9 - h) % RING, RING - h)
                    send(
                        self.emine.at[a], self.emine.at[b],
                        long_way if way == "L" else short_way,
                        self.sent_hop, self.hop_sem[way][h - 1],
                    )
            if h <= 5:
                for k in {h - 1, (9 - h) % RING} if h <= 4 else {4}:
                    self.swap_extra(k)

        def collect(self):
            for k in ORDER:
                arrived = self.rx.at[k] if k else self.rx.at[0, pl.ds(1, 3)]
                wait_for(arrived, self.main_sem[k])
                self.unpack(self.rx.at[k], k * 32)
            wait_for(self.epart, self.part_sem)
            for k in range(RING):
                self.unpack(self.emine.at[k], 256 + k * 16)
                self.unpack(self.epart.at[k], 384 + k * 16)

    def unpack_b(src, row):
        count = src.shape[0]
        values = src[...].astype(F32).reshape(count, 2, 8, width)
        rows = pl.ds(row, count * 8)
        x_b[rows, :] = values[:, 0].reshape(count * 8, width).astype(BF)
        s_b[rows, :] = values[:, 1].reshape(count * 8, width).astype(BF)

    def unpack_a(src, row):
        count = src.shape[0]
        values = src[...].astype(F32).reshape(count, 2, 8, half)
        rows = pl.ds(row, count * 8)
        x_a[rows, 0:half] = values[:, 0].reshape(count * 8, half).astype(BF)
        x_a[rows, half:] = values[:, 1].reshape(count * 8, half).astype(BF)

    def tile_at(i):
        return pl.ds(pl.multiple_of(i * TILE, TILE), TILE)

    def forward_units(i):
        cols = tile_at(i)
        gate_pre = dot(x_a[...], wg[:, cols])
        up_pre = dot(x_a[...], wu[:, cols])
        hid1[:, cols] = (gate_pre * jax.nn.sigmoid(gate_pre) * up_pre).astype(BF)

    def backward_units(i):
        cols = tile_at(i)
        gate_pre = dot(x_b[...], wg[:, cols])
        up_pre = dot(x_b[...], wu[:, cols])
        d_hidden = last_dot(s_b[...], wd[cols, :])
        sigma = jax.nn.sigmoid(gate_pre)
        hid1[:, cols] = (d_hidden * up_pre * sigma * (1.0 + gate_pre * (1.0 - sigma))).astype(BF)
        hid2[:, cols] = (d_hidden * gate_pre * sigma).astype(BF)

    def store_out(out, oute, hot, i, low, high):
        valid = jnp.broadcast_to(hot[28:29, :], (256, TILE)) > 8.5
        both = []
        for half_rows in (low, high):
            extra = jnp.where(valid, half_rows[256:512], 0.0)
            both.append(
                jnp.concatenate([half_rows[0:256], extra], axis=0).reshape(64, 8, TILE)
            )
        rows = jnp.concatenate(both, axis=1).astype(BF)
        oute[:, :, tile_at(i)] = rows[32:64]
        wide = out.shape[3]
        if out.shape[0] == 1:
            out[0, :, :, tile_at(i)] = rows[0:32]
        else:
            for j in range(TILE // wide):
                out[i * (TILE // wide) + j] = rows[0:32, :, j * wide:(j + 1) * wide]

    def shifted(base, i):
        return pl.ds(pl.multiple_of(base + i * TILE, TILE), TILE)

    def forward_out(i):
        low = dot(hid1[...], wd[:, shifted(0, i)])
        high = dot(hid1[...], wd[:, shifted(half, i)])
        store_out(out_a, oute_a, hot_a, i, low, high)

    def backward_out(i):
        now, later = shifted(0, i), shifted(half, i)
        low = last_dot(hid1[...], wg[now, :]) + last_dot(hid2[...], wu[now, :])
        high = last_dot(hid1[...], wg[later, :]) + last_dot(hid2[...], wu[later, :])
        store_out(out_b, oute_b, hot_b, i, low, high)

    def run(step, first, last):
        @pl.loop(first, last)
        def _(i):
            step(i)

    class Return:
        def __init__(self, parts, out, oute, epin, chain, etot, ein, fin):
            self.parts, self.out, self.oute = parts, out, oute
            self.epin, self.chain = epin, chain
            self.etot, self.ein, self.fin = etot, ein, fin
            self.main_sem = semaphores(len(parts))
            self.hop_sem = {"L": semaphores(4), "S": semaphores(3)}
            self.swap_sem, self.last_sem = semaphores(2)
            self.sent_main, self.sent_hop, self.sent_swap, self.sent_last = semaphores(4)
            unwaited.extend([
                (fin, self.sent_main), (chain, self.sent_hop), (epin, self.sent_swap),
                (ein, self.sent_last),
            ])

        def launch(self, part, blocks):
            for k, q in blocks:
                i = 4 * k + q
                send(
                    self.out.at[part, i], self.fin.at[part, i - 1], source(k, q),
                    self.sent_main, self.main_sem[part],
                )

        def swap(self):
            send(
                self.oute.at[pl.ds(16, 16)], self.epin, partner[1], self.sent_swap, self.swap_sem
            )

        def hop(self, way, h, src, dst):
            send(
                src, dst, short_way if way == "L" else long_way,
                self.sent_hop, self.hop_sem[way][h - 1],
            )

        def extra(self, h):
            if h == 1:
                wait_for(self.epin, self.swap_sem)
                mine = self.oute[0:16].astype(F32)
                self.epin[...] = (mine + self.epin[...].astype(F32)).astype(BF)
                self.hop("L", 1, self.epin.at[pl.ds(8, 2)], self.chain.at[0])
                self.hop("S", 1, self.epin.at[pl.ds(10, 2)], self.chain.at[4])
                return
            for way, last in EXTRA_HOPS.items():
                if h > last:
                    continue
                k, at = (5 - h, h - 2) if way == "L" else (4 + h, 2 + h)
                wait_for(self.chain.at[at], self.hop_sem[way][h - 2])
                mine = self.epin[2 * k:2 * k + 2].astype(F32)
                self.chain[at] = (self.chain[at].astype(F32) + mine).astype(BF)
                self.hop(way, h, self.chain.at[at], self.chain.at[at + 1])

        def finish_extra(self):
            wait_for(self.chain.at[3], self.hop_sem["L"][3])
            wait_for(self.chain.at[6], self.hop_sem["S"][2])
            total = self.epin[0:2].astype(F32) + self.chain[3].astype(F32)
            self.etot[...] = (total + self.chain[6].astype(F32)).astype(BF)
            send(self.etot.at[1], self.ein, partner[2], self.sent_last, self.last_sem)

        def collect_extra(self):
            wait_for(self.ein, self.last_sem)
            own, other = self.etot[0].astype(F32), self.ein[...].astype(F32)
            ret[256:272, 0:half] = jnp.concatenate([own[0:8], other[0:8]], axis=0).astype(BF)
            ret[256:272, half:] = jnp.concatenate([own[8:16], other[8:16]], axis=0).astype(BF)

        def collect(self, part):
            start, end = self.parts[part]
            wide = end - start
            cols = pl.ds(start, wide)
            wait_for(self.fin.at[part], self.main_sem[part])
            for k in range(RING):
                if k == 0:
                    own = self.out[part, 0:1].astype(F32)
                    block = jnp.concatenate([own, self.fin[part, 0:3].astype(F32)], axis=0)
                else:
                    block = self.fin[part, 4 * k - 1:4 * k + 3].astype(F32)
                block = block.reshape(4, 2, 8, wide)
                rows = pl.ds(PLACE[k] * 32, 32)
                ret[rows, cols] = block[:, 0].reshape(32, wide).astype(BF)
                ret[rows, pl.ds(half + start, wide)] = block[:, 1].reshape(32, wide).astype(BF)

    dis_a = Dispatch(send1_a, rx_a, esend_a, emine_a, epart_a, unpack_a)
    dis_b = Dispatch(send1_b, rx_b, esend_b, emine_b, epart_b, unpack_b)
    parts = [(i * half // PARTS_A, (i + 1) * half // PARTS_A) for i in range(PARTS_A)]
    ret_a = Return(parts, out_a, oute_a, epin_a, chain_a, etot_a, ein_a, fin_a)
    ret_b = Return([(0, half)], out_b, oute_b, epin_b, chain_b, etot_b, ein_b, fin_b)
    cut = chunks(6)
    tiles = ff // TILE
    step = min(512, half)

    for copy in got_b:
        copy.wait()
    routing(ids_b, dd_b, ddt_b, hot_b)
    gates(probs_b, gates_b)
    prepare(hid_b, gates_b, grad_b)
    pack(dd_b, send1_b, rx_b, emine_b, esend_b, columns(nn, 0), columns(gg, 0), width)
    pl.semaphore_wait(barrier, len(greeted))
    dis_b.start_extra()
    dis_b.launch(cut[0])

    for copy in got_a:
        copy.wait()
    routing(ids_a, dd_a, ddt_a, hot_a)
    gates(probs_a, gates_a)
    prepare(hid_a, gates_a, None)
    pack(dd_a, send1_a, rx_a, emine_a, esend_a, columns(nn, 0), columns(nn, half), half)
    ret[272:384, :] = jnp.zeros((112, width), BF)
    prev_sent, prev_got, next_sent, next_got, zero_sem = semaphores(5)

    def blank(ref):
        nn[0:tokens, :] = jnp.zeros((tokens, width), BF)
        pltpu.make_async_copy(nn.at[pl.ds(0, tokens)], ref, zero_sem).start()
        pltpu.make_async_copy(nn.at[pl.ds(0, tokens)], ref, zero_sem).wait()

    @pl.when(pipe == 0)
    def _():
        blank(next_ref)

    @pl.when(pipe == pipes - 1)
    def _():
        blank(prev_ref)

    dis_b.extra(1)
    dis_a.start_extra()
    dis_b.launch(cut[1])
    for h in range(2, 6):
        dis_b.extra(h)
        dis_a.extra(h - 1)
        dis_b.launch(cut[h])
    dis_a.launch(BLOCKS[:10])
    dis_a.extra(5)
    dis_a.launch(BLOCKS[10:])

    dis_b.collect()
    for copy in weights:
        copy.wait()
    run(backward_units, 0, tiles)
    run(backward_out, 0, half // TILE)
    ret_b.swap()
    ret_b.launch(0, BLOCKS[:8])
    dis_a.collect()
    ret_b.launch(0, BLOCKS[8:14])
    run(forward_units, 0, tiles)
    run(forward_out, 0, half // TILE)
    ret_a.swap()
    for h, (start, end) in enumerate(((14, 20), (20, 26), (26, 31), (31, 31))):
        ret_b.extra(h + 1)
        ret_a.extra(h + 1)
        ret_b.launch(0, BLOCKS[start:end])
    ret_a.launch(0, BLOCKS)
    ret_b.finish_extra()
    ret_a.finish_extra()
    for part in range(1, len(parts)):
        ret_a.launch(part, BLOCKS)

    ret_b.collect_extra()
    ret_b.collect(0)

    @pl.loop(0, width // step)
    def _(i):
        cols = pl.ds(pl.multiple_of(i * step, step), step)
        moved = dot(ddt_b[...], ret[:, cols])
        dnorm[:, cols] = moved[0:tokens] + moved[tokens:]

    @pl.loop(0, tokens // 16)
    def _(i):
        rows = pl.ds(pl.multiple_of(i * 16, 16), 16)
        values = hid_b[rows, :].astype(F32)
        r = inverse_norm(values)
        scaled = dnorm[rows, :] * gain_ref[...]
        inner = jnp.mean(values * scaled, axis=-1, keepdims=True)
        grown = grad_b[rows, :].astype(F32) + r * scaled - values * (r * r * r * inner)
        pipe_b[rows, :] = grown.astype(BF)

    if pipes > 1:
        @pl.when(pipe > 0)
        def _():
            send(pipe_b, prev_ref, pipe_prev, prev_sent, prev_got)

    ret_a.collect_extra()
    for part, (start, end) in enumerate(parts):
        ret_a.collect(part)
        for base in (start, half + start):
            cols = pl.ds(base, end - start)
            moved = dot(ddt_a[...], ret[:, cols])
            summed = gates_a[0, :, 0:1] * moved[0:tokens] + gates_a[1, :, 0:1] * moved[tokens:]
            pipe_a[:, cols] = (hid_a[:, cols].astype(F32) + summed).astype(BF)
        if pipes > 1:
            @pl.when(pipe < pipes - 1)
            def _():
                for base in (start, half + start):
                    cols = pl.ds(base, end - start)
                    send(
                        pipe_a.at[:, cols], next_ref.at[:, cols], pipe_next, next_sent, next_got
                    )

    for ref, sem in unwaited:
        wait_for(ref, sem)
    if pipes > 1:
        @pl.when(pipe < pipes - 1)
        def _():
            wait_for(prev_ref, prev_got)
            wait_for(pipe_a, next_sent)

        @pl.when(pipe > 0)
        def _():
            wait_for(pipe_b, prev_sent)
            wait_for(next_ref, next_got)


def hand_over(first, second, first_out, second_out, held, sems):
    moves = []
    for n, (source, result) in enumerate(((first, first_out), (second, second_out))):
        for i in range(2):
            rows = pl.ds(i * 64, 64)
            here = held.at[n, rows]
            moves.append((
                pltpu.make_async_copy(source.at[rows], here, sems.at[0, n, i]),
                pltpu.make_async_copy(here, result.at[rows], sems.at[1, n, i]),
            ))
    for fetch, _ in moves:
        fetch.start()
    for fetch, store in moves:
        fetch.wait()
        store.start()
    for _, store in moves:
        store.wait()


def scratch(tokens, width, ff):
    half = width // 2
    vmem = pltpu.VMEM
    shapes = [
        ((width, ff), BF), ((width, ff), BF), ((ff, width), BF),
        ((2 * tokens, width), BF), ((2 * tokens, width), BF),
        ((384, 2 * tokens), BF), ((384, 2 * tokens), BF),
        ((2 * tokens, 384), BF), ((2 * tokens, 384), BF),
        ((32, TILE), F32), ((32, TILE), F32),
        ((2, tokens, tokens), F32), ((2, tokens, tokens), F32),
        ((8, 4, 16, half), BF), ((8, 4, 16, width), BF),
        ((8, 4, 16, half), BF), ((8, 4, 16, width), BF),
        ((16, half), BF), ((16, width), BF),
        ((8, 2, 16, half), BF), ((8, 2, 16, width), BF),
        ((8, 2, 16, half), BF), ((8, 2, 16, width), BF),
        ((512, width), BF), ((512, width), BF), ((512, width), BF),
        ((512, ff), BF), ((512, ff), BF),
        ((PARTS_A, 32, 16, half // PARTS_A), BF), ((1, 32, 16, half), BF),
        ((32, 16, half), BF), ((32, 16, half), BF),
        ((16, 16, half), BF), ((16, 16, half), BF),
        ((7, 2, 16, half), BF), ((7, 2, 16, half), BF),
        ((2, 16, half), BF), ((2, 16, half), BF),
        ((16, half), BF), ((16, half), BF),
        ((PARTS_A, 31, 16, half // PARTS_A), BF), ((1, 31, 16, half), BF),
        ((384, width), BF), ((tokens, width), F32),
        ((tokens, width), BF), ((tokens, width), BF),
    ]
    arguments = [
        ((8, tokens), jnp.int32), ((8, tokens), jnp.int32), ((8, tokens), F32), ((8, tokens), F32),
        ((tokens, width), BF), ((tokens, width), BF), ((tokens, width), BF), ((1, width), F32),
    ]
    return [vmem(shape, kind) for shape, kind in arguments + shapes] + [
        pltpu.SemaphoreType.DMA((SEMAPHORES,))
    ]


def per_device(
    hidden_a, expert_ids_a, router_probs_a, hidden_b, expert_ids_b, router_probs_b,
    grad_out_b, norm_gain, w_gate, w_up, w_down,
):
    tokens, width = hidden_a.shape[1:]
    ff = w_gate.shape[3]
    small = [
        jnp.swapaxes(value[0], 0, 1)
        for value in (expert_ids_a, expert_ids_b, router_probs_a, router_probs_b)
    ]
    outside = pl.BlockSpec(memory_space=pl.ANY)
    result = jax.ShapeDtypeStruct((tokens, width), BF)
    rows = 512
    next_hidden, grad_before = pl.pallas_call(
        kernel,
        out_shape=(result, result),
        in_specs=[outside] * 11,
        out_specs=(outside, outside),
        scratch_shapes=scratch(tokens, width, ff),
        compiler_params=pltpu.CompilerParams(
            collective_id=0, has_side_effects=True, vmem_limit_bytes=60 * 1024 * 1024
        ),
        cost_estimate=pl.CostEstimate(
            flops=2 * rows * width * ff * 8, bytes_accessed=6 * width * ff, transcendentals=0
        ),
    )(
        *small, hidden_a[0], hidden_b[0], grad_out_b[0],
        norm_gain, w_gate[0, 0], w_up[0, 0], w_down[0, 0],
    )
    next_hidden, grad_before = pl.pallas_call(
        hand_over,
        out_shape=(result, result),
        in_specs=[outside] * 2,
        out_specs=(outside, outside),
        scratch_shapes=[pltpu.VMEM((2, tokens, width), BF), pltpu.SemaphoreType.DMA((2, 2, 2))],
    )(next_hidden, grad_before)
    return next_hidden[None], grad_before[None]


def solution(mesh):
    in_specs = (
        P("pipe", "expert", None),
        P("pipe", "expert", None),
        P("pipe", "expert", None),
        P("pipe", "expert", None),
        P("pipe", "expert", None),
        P("pipe", "expert", None),
        P("pipe", "expert", None),
        P("pipe", None),
        P("pipe", "expert", None, None),
        P("pipe", "expert", None, None),
        P("pipe", "expert", None, None),
    )
    out_specs = (P("pipe", "expert", None), P("pipe", "expert", None))
    return jax.shard_map(
        per_device, mesh=mesh, in_specs=in_specs, out_specs=out_specs, check_vma=False
    )
```

```python
import jax
import jax.numpy as jnp
from jax import lax
from jax.experimental import pallas as pl
from jax.experimental.pallas import tpu as pltpu
from jax.sharding import PartitionSpec as P

NORM_EPS = 1e-06
MESH = pl.DeviceIdType.MESH
BF = jnp.bfloat16
F32 = jnp.float32
RING = 8
ORDER = (4, 3, 5, 2, 6, 1, 7, 0)
PLACE = {k: s for s, k in enumerate(ORDER)}
TILE = 256
PARTS_A = 8
BLOCKS = [(k, q) for k in ORDER for q in (2, 3, 0, 1) if (k, q) != (0, 0)]
SEMAPHORES = 96
EXTRA_HOPS = {"L": 4, "S": 3}


def chunks(count):
    size = -(-len(BLOCKS) // count)
    return [BLOCKS[i:i + size] for i in range(0, len(BLOCKS), size)]


def last_dot(left, right):
    return lax.dot_general(left, right, (((1,), (1,)), ((), ())), preferred_element_type=F32)


def dot(left, right):
    return jnp.dot(left, right, preferred_element_type=F32)


def kernel(
    ids_a_hbm, ids_b_hbm, probs_a_hbm, probs_b_hbm, hid_a_hbm, hid_b_hbm, grad_b_hbm, gain_hbm,
    wg_hbm, wu_hbm, wd_hbm,
    next_ref, prev_ref,
    ids_a, ids_b, probs_a, probs_b, hid_a, hid_b, grad_b, gain_ref, wg, wu, wd, nn, gg, dd_a, dd_b, ddt_a, ddt_b, hot_a, hot_b, gates_a, gates_b,
    send1_a, send1_b, rx_a, rx_b, esend_a, esend_b, emine_a, emine_b, epart_a, epart_b,
    x_a, x_b, s_b, hid1, hid2, out_a, out_b, oute_a, oute_b, epin_a, epin_b,
    chain_a, chain_b, etot_a, etot_b, ein_a, ein_b, fin_a, fin_b,
    ret, dnorm, pipe_a, pipe_b, sems,
):
    pipe = lax.axis_index("pipe")
    pipes = lax.axis_size("pipe")
    me = lax.axis_index("expert")
    core = lax.rem(me, 2)
    z = lax.rem(lax.div(me, 2), RING)
    x = lax.div(me, 2 * RING)
    sg = 1 - 2 * core
    width = hid_a.shape[1]
    half = width // 2
    ff = wg.shape[1]
    tokens = hid_a.shape[0]

    def device(xx, zz, cc):
        return {"expert": (xx * RING + zz) * 2 + cc}

    partner = [
        device(x if q < 2 else 1 - x, z, core if q % 2 == 0 else 1 - core) for q in range(4)
    ]

    def target(k, q):
        cc = core if q % 2 == 0 else 1 - core
        return device(x if q < 2 else 1 - x, lax.rem(z + (1 - 2 * cc) * k + RING, RING), cc)

    def source(k, q):
        cc = core if q % 2 == 0 else 1 - core
        return device(x if q < 2 else 1 - x, lax.rem(z - sg * k + RING, RING), cc)

    long_way = device(x, lax.rem(z + sg + RING, RING), core)
    short_way = device(x, lax.rem(z - sg + RING, RING), core)
    pipe_next = {"pipe": lax.rem(pipe + 1, pipes)}
    pipe_prev = {"pipe": lax.rem(pipe + pipes - 1, pipes)}

    used = [0]
    unwaited = []

    def semaphores(count):
        first = used[0]
        used[0] += count
        return [sems.at[first + i] for i in range(count)]

    def wait_for(ref, sem):
        pltpu.make_async_copy(ref, ref, sem).wait()

    def send(src, dst, where, send_sem, recv_sem):
        copy = pltpu.make_async_remote_copy(
            src_ref=src, dst_ref=dst, send_sem=send_sem, recv_sem=recv_sem,
            device_id=where, device_id_type=MESH,
        )
        copy.start()

    barrier = pltpu.get_barrier_semaphore()
    greeted = [target(k, q) for k, q in BLOCKS]
    if pipes > 1:
        greeted += [pipe_next, pipe_prev]
    for other in greeted:
        pl.semaphore_signal(barrier, inc=1, device_id=other, device_id_type=MESH)

    def fetch(src, dst):
        copy = pltpu.make_async_copy(src, dst, semaphores(1)[0])
        copy.start()
        return copy

    got_b = [
        fetch(*pair) for pair in (
            (ids_b_hbm, ids_b), (probs_b_hbm, probs_b), (gain_hbm, gain_ref),
            (hid_b_hbm, hid_b), (grad_b_hbm, grad_b),
        )
    ]
    got_a = [
        fetch(*pair) for pair in ((ids_a_hbm, ids_a), (probs_a_hbm, probs_a), (hid_a_hbm, hid_a))
    ]
    weights = [fetch(*pair) for pair in ((wg_hbm, wg), (wu_hbm, wu), (wd_hbm, wd))]

    def routing(ids_ref, dd, ddt, hot):
        ids = ids_ref[...]
        j = lax.broadcasted_iota(jnp.int32, (32, tokens), 0)
        q = j & 3
        s = j >> 2
        k = jnp.where((s & 1) == 1, 3 - (s >> 1), 4 + (s >> 1))
        cq = (core + (q & 1)) & 1
        xq = (x + (q >> 1)) & 1
        zq = (z + (1 - 2 * cq) * k + RING) & (RING - 1)
        expert = (xq * RING + zq) * 2 + cq
        match = (ids[0:1, :] == expert) | (ids[1:2, :] == expert)
        matched = jnp.where(match, 1.0, 0.0)
        t0 = lax.broadcasted_iota(jnp.int32, (tokens, tokens), 0)
        t1 = lax.broadcasted_iota(jnp.int32, (tokens, tokens), 1)
        rank = dot(matched.astype(BF), jnp.where(t0 < t1, 1.0, 0.0).astype(BF))
        ranked = jnp.where(match, rank, 200.0)
        own = q < 2
        rank_own = jnp.sum(jnp.where(own, matched * rank, 0.0), axis=0, keepdims=True)
        rank_other = jnp.sum(jnp.where(own, 0.0, matched * rank), axis=0, keepdims=True)
        hot[...] = dot(matched.astype(BF), jnp.ones((tokens, TILE), BF))
        r = lax.broadcasted_iota(jnp.int32, (256, 32), 0)
        cols = lax.broadcasted_iota(jnp.int32, (256, 32), 1)
        spread = jnp.where((r >> 3) == cols, 1.0, 0.0).astype(BF)
        rows = dot(spread, ranked.astype(BF))
        r = lax.broadcasted_iota(jnp.int32, (256, tokens), 0)
        hit = rows == (r & 7).astype(F32)
        mine = ((r >> 3) & 3) < 2
        dd[0:256, 0:tokens] = jnp.where(hit & mine, 1.0, 0.0).astype(BF)
        dd[0:256, tokens:] = jnp.where(hit & jnp.logical_not(mine), 1.0, 0.0).astype(BF)
        r = lax.broadcasted_iota(jnp.int32, (128, tokens), 0)
        rf = r.astype(F32)
        dd[256:384, 0:tokens] = jnp.where((rank_own == rf + 8.0) & (r < 8), 1.0, 0.0).astype(BF)
        dd[256:384, tokens:] = jnp.where(
            (rank_other == rf) & (r >= 8) & (r < 16), 1.0, 0.0
        ).astype(BF)
        t0 = lax.broadcasted_iota(jnp.int32, (2 * tokens, 2 * tokens), 0)
        t1 = lax.broadcasted_iota(jnp.int32, (2 * tokens, 2 * tokens), 1)
        eye = jnp.where(t0 == t1, 1.0, 0.0).astype(BF)
        ddt[...] = last_dot(eye, dd[...]).astype(BF)

    xf = x.astype(F32)

    def gates(probs_ref, gate):
        probs = probs_ref[...]
        weight = probs / jnp.sum(probs, axis=0, keepdims=True)
        first, second = weight[0:1, :], weight[1:2, :]
        for i, row in enumerate(
            (first * (1.0 - xf) + second * xf, second * (1.0 - xf) + first * xf)
        ):
            gate[i] = jnp.broadcast_to(row, (tokens, tokens)).T

    def inverse_norm(values):
        return lax.rsqrt(jnp.mean(values * values, axis=-1, keepdims=True) + NORM_EPS)

    def prepare(hidden, gate, gradient):
        @pl.loop(0, tokens // 16)
        def _(i):
            rows = pl.ds(pl.multiple_of(i * 16, 16), 16)
            later = pl.ds(pl.multiple_of(tokens + i * 16, 16), 16)
            values = hidden[rows, :].astype(F32)
            normed = (values * inverse_norm(values) * gain_ref[...]).astype(BF)
            nn[rows, :] = normed
            nn[later, :] = normed
            if gradient is not None:
                up = gradient[rows, :].astype(F32)
                gg[rows, :] = (gate[0, rows, 0:1] * up).astype(BF)
                gg[later, :] = (gate[1, rows, 0:1] * up).astype(BF)

    def pack(dd, send1, rx, emine, esend, first, second, wide):
        step = min(512, wide)

        @pl.loop(0, wide // step)
        def _(i):
            cols = pl.ds(pl.multiple_of(i * step, step), step)
            top = dot(dd[0:272, :], first(i * step, step))
            low = dot(dd[0:272, :], second(i * step, step))
            both = jnp.concatenate(
                [top.reshape(34, 8, step), low.reshape(34, 8, step)], axis=1
            ).astype(BF)
            send1[:, :, :, cols] = both[0:32].reshape(8, 4, 16, step)
            rx[0, 0, :, cols] = both[4 * PLACE[0]]
            emine[0, 0, :, cols] = both[32]
            esend[:, cols] = both[33]

    def columns(ref, base):
        def take(start, size):
            return ref[:, pl.ds(pl.multiple_of(base + start, size), size)]

        return take

    class Dispatch:
        def __init__(self, send1, rx, esend, emine, epart, unpack):
            self.send1, self.rx, self.esend, self.emine = send1, rx, esend, emine
            self.epart, self.unpack = epart, unpack
            self.main_sem = semaphores(RING)
            self.hop_sem = {"L": semaphores(4), "S": semaphores(3)}
            self.first_sem, self.part_sem = semaphores(2)
            self.sent_first, self.sent_hop, self.sent_part = semaphores(3)
            self.sent_far, self.sent_near = semaphores(2)
            unwaited.extend([
                (rx.at[pl.ds(1, 7)], self.sent_far), (rx.at[0, pl.ds(1, 3)], self.sent_near),
                (esend, self.sent_first), (emine.at[pl.ds(0, 7)], self.sent_hop),
                (emine, self.sent_part),
            ])

        def launch(self, blocks):
            for k, q in blocks:
                send(
                    self.send1.at[PLACE[k], q], self.rx.at[k, q], target(k, q),
                    self.sent_far if k else self.sent_near, self.main_sem[k],
                )

        def start_extra(self):
            send(self.esend, self.emine.at[0, 1], partner[2], self.sent_first, self.first_sem)

        def swap_extra(self, k):
            send(self.emine.at[k], self.epart.at[k], partner[1], self.sent_part, self.part_sem)

        def extra(self, h):
            if h == 1:
                wait_for(self.emine.at[0, 1], self.first_sem)
            for way, last in EXTRA_HOPS.items():
                if 1 < h <= last + 1:
                    wait_for(self.emine.at[0], self.hop_sem[way][h - 2])
                if h <= last:
                    a, b = (h - 1, h) if way == "L" else ((9 - h) % RING, RING - h)
                    send(
                        self.emine.at[a], self.emine.at[b],
                        long_way if way == "L" else short_way,
                        self.sent_hop, self.hop_sem[way][h - 1],
                    )
            if h <= 5:
                for k in {h - 1, (9 - h) % RING} if h <= 4 else {4}:
                    self.swap_extra(k)

        def collect(self):
            for k in ORDER:
                arrived = self.rx.at[k] if k else self.rx.at[0, pl.ds(1, 3)]
                wait_for(arrived, self.main_sem[k])
                self.unpack(self.rx.at[k], k * 32)
            wait_for(self.epart, self.part_sem)
            for k in range(RING):
                self.unpack(self.emine.at[k], 256 + k * 16)
                self.unpack(self.epart.at[k], 384 + k * 16)

    def unpack_b(src, row):
        count = src.shape[0]
        values = src[...].astype(F32).reshape(count, 2, 8, width)
        rows = pl.ds(row, count * 8)
        x_b[rows, :] = values[:, 0].reshape(count * 8, width).astype(BF)
        s_b[rows, :] = values[:, 1].reshape(count * 8, width).astype(BF)

    def unpack_a(src, row):
        count = src.shape[0]
        values = src[...].astype(F32).reshape(count, 2, 8, half)
        rows = pl.ds(row, count * 8)
        x_a[rows, 0:half] = values[:, 0].reshape(count * 8, half).astype(BF)
        x_a[rows, half:] = values[:, 1].reshape(count * 8, half).astype(BF)

    def tile_at(i):
        return pl.ds(pl.multiple_of(i * TILE, TILE), TILE)

    def forward_units(i):
        cols = tile_at(i)
        gate_pre = dot(x_a[...], wg[:, cols])
        up_pre = dot(x_a[...], wu[:, cols])
        hid1[:, cols] = (gate_pre * jax.nn.sigmoid(gate_pre) * up_pre).astype(BF)

    def backward_units(i):
        cols = tile_at(i)
        gate_pre = dot(x_b[...], wg[:, cols])
        up_pre = dot(x_b[...], wu[:, cols])
        d_hidden = last_dot(s_b[...], wd[cols, :])
        sigma = jax.nn.sigmoid(gate_pre)
        hid1[:, cols] = (d_hidden * up_pre * sigma * (1.0 + gate_pre * (1.0 - sigma))).astype(BF)
        hid2[:, cols] = (d_hidden * gate_pre * sigma).astype(BF)

    def store_out(out, oute, hot, i, low, high):
        valid = jnp.broadcast_to(hot[28:29, :], (256, TILE)) > 8.5
        both = []
        for half_rows in (low, high):
            extra = jnp.where(valid, half_rows[256:512], 0.0)
            both.append(
                jnp.concatenate([half_rows[0:256], extra], axis=0).reshape(64, 8, TILE)
            )
        rows = jnp.concatenate(both, axis=1).astype(BF)
        oute[:, :, tile_at(i)] = rows[32:64]
        wide = out.shape[3]
        if out.shape[0] == 1:
            out[0, :, :, tile_at(i)] = rows[0:32]
        else:
            for j in range(TILE // wide):
                out[i * (TILE // wide) + j] = rows[0:32, :, j * wide:(j + 1) * wide]

    def shifted(base, i):
        return pl.ds(pl.multiple_of(base + i * TILE, TILE), TILE)

    def forward_out(i):
        low = dot(hid1[...], wd[:, shifted(0, i)])
        high = dot(hid1[...], wd[:, shifted(half, i)])
        store_out(out_a, oute_a, hot_a, i, low, high)

    def backward_out(i):
        now, later = shifted(0, i), shifted(half, i)
        low = last_dot(hid1[...], wg[now, :]) + last_dot(hid2[...], wu[now, :])
        high = last_dot(hid1[...], wg[later, :]) + last_dot(hid2[...], wu[later, :])
        store_out(out_b, oute_b, hot_b, i, low, high)

    def run(step, first, last):
        @pl.loop(first, last)
        def _(i):
            step(i)

    class Return:
        def __init__(self, parts, out, oute, epin, chain, etot, ein, fin):
            self.parts, self.out, self.oute = parts, out, oute
            self.epin, self.chain = epin, chain
            self.etot, self.ein, self.fin = etot, ein, fin
            self.main_sem = semaphores(len(parts))
            self.hop_sem = {"L": semaphores(4), "S": semaphores(3)}
            self.swap_sem, self.last_sem = semaphores(2)
            self.sent_main, self.sent_hop, self.sent_swap, self.sent_last = semaphores(4)
            unwaited.extend([
                (fin, self.sent_main), (chain, self.sent_hop), (epin, self.sent_swap),
                (ein, self.sent_last),
            ])

        def launch(self, part, blocks):
            for k, q in blocks:
                i = 4 * k + q
                send(
                    self.out.at[part, i], self.fin.at[part, i - 1], source(k, q),
                    self.sent_main, self.main_sem[part],
                )

        def swap(self):
            send(
                self.oute.at[pl.ds(16, 16)], self.epin, partner[1], self.sent_swap, self.swap_sem
            )

        def hop(self, way, h, src, dst):
            send(
                src, dst, short_way if way == "L" else long_way,
                self.sent_hop, self.hop_sem[way][h - 1],
            )

        def extra(self, h):
            if h == 1:
                wait_for(self.epin, self.swap_sem)
                mine = self.oute[0:16].astype(F32)
                self.epin[...] = (mine + self.epin[...].astype(F32)).astype(BF)
                self.hop("L", 1, self.epin.at[pl.ds(8, 2)], self.chain.at[0])
                self.hop("S", 1, self.epin.at[pl.ds(10, 2)], self.chain.at[4])
                return
            for way, last in EXTRA_HOPS.items():
                if h > last:
                    continue
                k, at = (5 - h, h - 2) if way == "L" else (4 + h, 2 + h)
                wait_for(self.chain.at[at], self.hop_sem[way][h - 2])
                mine = self.epin[2 * k:2 * k + 2].astype(F32)
                self.chain[at] = (self.chain[at].astype(F32) + mine).astype(BF)
                self.hop(way, h, self.chain.at[at], self.chain.at[at + 1])

        def finish_extra(self):
            wait_for(self.chain.at[3], self.hop_sem["L"][3])
            wait_for(self.chain.at[6], self.hop_sem["S"][2])
            total = self.epin[0:2].astype(F32) + self.chain[3].astype(F32)
            self.etot[...] = (total + self.chain[6].astype(F32)).astype(BF)
            send(self.etot.at[1], self.ein, partner[2], self.sent_last, self.last_sem)

        def collect_extra(self):
            wait_for(self.ein, self.last_sem)
            own, other = self.etot[0].astype(F32), self.ein[...].astype(F32)
            ret[256:272, 0:half] = jnp.concatenate([own[0:8], other[0:8]], axis=0).astype(BF)
            ret[256:272, half:] = jnp.concatenate([own[8:16], other[8:16]], axis=0).astype(BF)

        def collect(self, part):
            start, end = self.parts[part]
            wide = end - start
            cols = pl.ds(start, wide)
            wait_for(self.fin.at[part], self.main_sem[part])
            for k in range(RING):
                if k == 0:
                    own = self.out[part, 0:1].astype(F32)
                    block = jnp.concatenate([own, self.fin[part, 0:3].astype(F32)], axis=0)
                else:
                    block = self.fin[part, 4 * k - 1:4 * k + 3].astype(F32)
                block = block.reshape(4, 2, 8, wide)
                rows = pl.ds(PLACE[k] * 32, 32)
                ret[rows, cols] = block[:, 0].reshape(32, wide).astype(BF)
                ret[rows, pl.ds(half + start, wide)] = block[:, 1].reshape(32, wide).astype(BF)

    dis_a = Dispatch(send1_a, rx_a, esend_a, emine_a, epart_a, unpack_a)
    dis_b = Dispatch(send1_b, rx_b, esend_b, emine_b, epart_b, unpack_b)
    parts = [(i * half // PARTS_A, (i + 1) * half // PARTS_A) for i in range(PARTS_A)]
    ret_a = Return(parts, out_a, oute_a, epin_a, chain_a, etot_a, ein_a, fin_a)
    ret_b = Return([(0, half)], out_b, oute_b, epin_b, chain_b, etot_b, ein_b, fin_b)
    cut = chunks(6)
    tiles = ff // TILE
    step = min(512, half)

    for copy in got_b:
        copy.wait()
    routing(ids_b, dd_b, ddt_b, hot_b)
    gates(probs_b, gates_b)
    prepare(hid_b, gates_b, grad_b)
    pack(dd_b, send1_b, rx_b, emine_b, esend_b, columns(nn, 0), columns(gg, 0), width)
    pl.semaphore_wait(barrier, len(greeted))
    dis_b.start_extra()
    dis_b.launch(cut[0])

    for copy in got_a:
        copy.wait()
    routing(ids_a, dd_a, ddt_a, hot_a)
    gates(probs_a, gates_a)
    prepare(hid_a, gates_a, None)
    pack(dd_a, send1_a, rx_a, emine_a, esend_a, columns(nn, 0), columns(nn, half), half)
    ret[272:384, :] = jnp.zeros((112, width), BF)
    prev_sent, prev_got, next_sent, next_got, zero_sem = semaphores(5)

    def blank(ref):
        nn[0:tokens, :] = jnp.zeros((tokens, width), BF)
        pltpu.make_async_copy(nn.at[pl.ds(0, tokens)], ref, zero_sem).start()
        pltpu.make_async_copy(nn.at[pl.ds(0, tokens)], ref, zero_sem).wait()

    @pl.when(pipe == 0)
    def _():
        blank(next_ref)

    @pl.when(pipe == pipes - 1)
    def _():
        blank(prev_ref)

    dis_b.extra(1)
    dis_a.start_extra()
    dis_b.launch(cut[1])
    for h in range(2, 6):
        dis_b.extra(h)
        dis_a.extra(h - 1)
        dis_b.launch(cut[h])
    dis_a.launch(BLOCKS[:10])
    dis_a.extra(5)
    dis_a.launch(BLOCKS[10:])

    dis_b.collect()
    for copy in weights:
        copy.wait()
    run(backward_units, 0, tiles)
    run(backward_out, 0, half // TILE)
    ret_b.swap()
    ret_b.launch(0, BLOCKS[:8])
    dis_a.collect()
    ret_b.launch(0, BLOCKS[8:16])
    run(forward_units, 0, tiles)
    run(forward_out, 0, half // TILE)
    ret_a.swap()
    for h, (start, end) in enumerate(((16, 21), (21, 26), (26, 31), (31, 31))):
        ret_b.extra(h + 1)
        ret_a.extra(h + 1)
        ret_b.launch(0, BLOCKS[start:end])
    ret_a.launch(0, BLOCKS)
    ret_b.finish_extra()
    ret_a.finish_extra()
    for part in range(1, len(parts)):
        ret_a.launch(part, BLOCKS)

    ret_b.collect_extra()
    ret_b.collect(0)

    @pl.loop(0, width // step)
    def _(i):
        cols = pl.ds(pl.multiple_of(i * step, step), step)
        moved = dot(ddt_b[...], ret[:, cols])
        dnorm[:, cols] = moved[0:tokens] + moved[tokens:]

    @pl.loop(0, tokens // 16)
    def _(i):
        rows = pl.ds(pl.multiple_of(i * 16, 16), 16)
        values = hid_b[rows, :].astype(F32)
        r = inverse_norm(values)
        scaled = dnorm[rows, :] * gain_ref[...]
        inner = jnp.mean(values * scaled, axis=-1, keepdims=True)
        grown = grad_b[rows, :].astype(F32) + r * scaled - values * (r * r * r * inner)
        pipe_b[rows, :] = grown.astype(BF)

    if pipes > 1:
        @pl.when(pipe > 0)
        def _():
            send(pipe_b, prev_ref, pipe_prev, prev_sent, prev_got)

    ret_a.collect_extra()
    for part, (start, end) in enumerate(parts):
        ret_a.collect(part)
        for base in (start, half + start):
            cols = pl.ds(base, end - start)
            moved = dot(ddt_a[...], ret[:, cols])
            summed = gates_a[0, :, 0:1] * moved[0:tokens] + gates_a[1, :, 0:1] * moved[tokens:]
            pipe_a[:, cols] = (hid_a[:, cols].astype(F32) + summed).astype(BF)
        if pipes > 1:
            @pl.when(pipe < pipes - 1)
            def _():
                for base in (start, half + start):
                    cols = pl.ds(base, end - start)
                    send(
                        pipe_a.at[:, cols], next_ref.at[:, cols], pipe_next, next_sent, next_got
                    )

    for ref, sem in unwaited:
        wait_for(ref, sem)
    if pipes > 1:
        @pl.when(pipe < pipes - 1)
        def _():
            wait_for(prev_ref, prev_got)
            wait_for(pipe_a, next_sent)

        @pl.when(pipe > 0)
        def _():
            wait_for(pipe_b, prev_sent)
            wait_for(next_ref, next_got)


def hand_over(first, second, first_out, second_out, held, sems):
    moves = []
    for n, (source, result) in enumerate(((first, first_out), (second, second_out))):
        for i in range(2):
            rows = pl.ds(i * 64, 64)
            here = held.at[n, rows]
            moves.append((
                pltpu.make_async_copy(source.at[rows], here, sems.at[0, n, i]),
                pltpu.make_async_copy(here, result.at[rows], sems.at[1, n, i]),
            ))
    for fetch, _ in moves:
        fetch.start()
    for fetch, store in moves:
        fetch.wait()
        store.start()
    for _, store in moves:
        store.wait()


def scratch(tokens, width, ff):
    half = width // 2
    vmem = pltpu.VMEM
    shapes = [
        ((width, ff), BF), ((width, ff), BF), ((ff, width), BF),
        ((2 * tokens, width), BF), ((2 * tokens, width), BF),
        ((384, 2 * tokens), BF), ((384, 2 * tokens), BF),
        ((2 * tokens, 384), BF), ((2 * tokens, 384), BF),
        ((32, TILE), F32), ((32, TILE), F32),
        ((2, tokens, tokens), F32), ((2, tokens, tokens), F32),
        ((8, 4, 16, half), BF), ((8, 4, 16, width), BF),
        ((8, 4, 16, half), BF), ((8, 4, 16, width), BF),
        ((16, half), BF), ((16, width), BF),
        ((8, 2, 16, half), BF), ((8, 2, 16, width), BF),
        ((8, 2, 16, half), BF), ((8, 2, 16, width), BF),
        ((512, width), BF), ((512, width), BF), ((512, width), BF),
        ((512, ff), BF), ((512, ff), BF),
        ((PARTS_A, 32, 16, half // PARTS_A), BF), ((1, 32, 16, half), BF),
        ((32, 16, half), BF), ((32, 16, half), BF),
        ((16, 16, half), BF), ((16, 16, half), BF),
        ((7, 2, 16, half), BF), ((7, 2, 16, half), BF),
        ((2, 16, half), BF), ((2, 16, half), BF),
        ((16, half), BF), ((16, half), BF),
        ((PARTS_A, 31, 16, half // PARTS_A), BF), ((1, 31, 16, half), BF),
        ((384, width), BF), ((tokens, width), F32),
        ((tokens, width), BF), ((tokens, width), BF),
    ]
    arguments = [
        ((8, tokens), jnp.int32), ((8, tokens), jnp.int32), ((8, tokens), F32), ((8, tokens), F32),
        ((tokens, width), BF), ((tokens, width), BF), ((tokens, width), BF), ((1, width), F32),
    ]
    return [vmem(shape, kind) for shape, kind in arguments + shapes] + [
        pltpu.SemaphoreType.DMA((SEMAPHORES,))
    ]


def per_device(
    hidden_a, expert_ids_a, router_probs_a, hidden_b, expert_ids_b, router_probs_b,
    grad_out_b, norm_gain, w_gate, w_up, w_down,
):
    tokens, width = hidden_a.shape[1:]
    ff = w_gate.shape[3]
    small = [
        jnp.swapaxes(value[0], 0, 1)
        for value in (expert_ids_a, expert_ids_b, router_probs_a, router_probs_b)
    ]
    outside = pl.BlockSpec(memory_space=pl.ANY)
    result = jax.ShapeDtypeStruct((tokens, width), BF)
    rows = 512
    next_hidden, grad_before = pl.pallas_call(
        kernel,
        out_shape=(result, result),
        in_specs=[outside] * 11,
        out_specs=(outside, outside),
        scratch_shapes=scratch(tokens, width, ff),
        compiler_params=pltpu.CompilerParams(
            collective_id=0, has_side_effects=True, vmem_limit_bytes=60 * 1024 * 1024
        ),
        cost_estimate=pl.CostEstimate(
            flops=2 * rows * width * ff * 8, bytes_accessed=6 * width * ff, transcendentals=0
        ),
    )(
        *small, hidden_a[0], hidden_b[0], grad_out_b[0],
        norm_gain, w_gate[0, 0], w_up[0, 0], w_down[0, 0],
    )
    next_hidden, grad_before = pl.pallas_call(
        hand_over,
        out_shape=(result, result),
        in_specs=[outside] * 2,
        out_specs=(outside, outside),
        scratch_shapes=[pltpu.VMEM((2, tokens, width), BF), pltpu.SemaphoreType.DMA((2, 2, 2))],
    )(next_hidden, grad_before)
    return next_hidden[None], grad_before[None]


def solution(mesh):
    in_specs = (
        P("pipe", "expert", None),
        P("pipe", "expert", None),
        P("pipe", "expert", None),
        P("pipe", "expert", None),
        P("pipe", "expert", None),
        P("pipe", "expert", None),
        P("pipe", "expert", None),
        P("pipe", None),
        P("pipe", "expert", None, None),
        P("pipe", "expert", None, None),
        P("pipe", "expert", None, None),
    )
    out_specs = (P("pipe", "expert", None), P("pipe", "expert", None))
    return jax.shard_map(
        per_device, mesh=mesh, in_specs=in_specs, out_specs=out_specs, check_vma=False
    )
```
